512 devices in a mesh: dp: 32 (over z, x_hi), mrow: 8 (over y, x_lo), mcol: 2 (over core).
Axes of the slice: x: 4 (x_hi: 2, x_lo: 2; x = x_hi * 2 + x_lo), y: 4, z: 16, core: 2. Of those that a mesh axis runs over, the one named last changes fastest.
Arguments:
- inputs: bfloat16 [32768, 8192], P('dp', 'mrow'), may hold values from -6 to 6
- kv_grads: bfloat16 [32768, 512], P('dp', 'mcol'), may hold values from -6 to 6
- weight: bfloat16 [8192, 512], P('mrow', 'mcol'), may hold values from -0.25 to 0.25
- master: float32 [8, 32, 32, 512], P('mrow', 'dp', None, 'mcol'), may hold values from -6 to 6
- row_state: float32 [2, 8, 32, 32], P('mcol', 'mrow', 'dp'), may hold values from 65.536 to 16384
- col_state: float32 [2, 256], P('mcol'), may hold values from 65.536 to 16384
Outputs:
- new_master: float32 [8, 32, 32, 512], P('mrow', 'dp', None, 'mcol')
- new_rows: float32 [2, 8, 32, 32], P('mcol', 'mrow', 'dp')
- new_cols: float32 [2, 256], P('mcol')
- new_weight: bfloat16 [8192, 512], P('mrow', 'mcol')
- input_grad: bfloat16 [32768, 8192], P('dp', ('mrow', 'mcol'))
The draws below stay inside these ranges and needn't reach their ends.
All inputs are finite; a program needn't handle non-finite values.
Results may differ from the reference program's by a relative error of at most 0.0051.
Values may be sent and summed in bfloat16 or wider, within the bound.
A program may use at most 64 MiB of HBM per device.

```python
import math
import jax
import jax.numpy as jnp
from jax import lax

D = 8192
HEAD = 256
KV = 512
TOKENS = 32768
SHARD = 32
N_DP = 32
N_MROW = 8


def rising_spread(key, lowest, highest):
    shape = (2, N_MROW, N_DP, SHARD)
    fraction = jax.random.uniform(key, shape, jnp.float32)
    along = jnp.arange(N_DP, dtype=jnp.float32) / jnp.float32(max(N_DP - 1, 1))
    level = 0.7 * along[None, None, :, None] + 0.3 * fraction
    return (lowest * jnp.exp(level * math.log(highest / lowest))).astype(jnp.float32)


def log_spread(key, shape, lowest, highest):
    fraction = jax.random.uniform(key, shape, jnp.float32)
    return (lowest * jnp.exp(fraction * math.log(highest / lowest))).astype(jnp.float32)


def draw_row_state(key, part):
    key = jax.random.fold_in(key, 11)
    return rising_spread(key, 0.005 * TOKENS, 0.3 * TOKENS)


def draw_col_state(key, part):
    key = jax.random.fold_in(key, 23)
    return log_spread(key, (2, HEAD), 0.005 * TOKENS, 0.05 * TOKENS)


def block_levels(key, extent, pieces, least, top_value):
    level = 1.0
    for position, parts in pieces:
        heights = jax.random.uniform(jax.random.fold_in(jax.random.fold_in(key, 6), position), (parts,), jnp.float32, least / len(pieces), top_value / len(pieces))
        level = level * jnp.repeat(jnp.exp(heights), extent[position] // parts).reshape((-1,) + (1,) * (len(extent) - 1 - position))
    return level


def normal_values(rng, dims, deviation, reach, split=(), held_as=jnp.bfloat16):
    array = deviation * jax.random.normal(rng, dims, jnp.float32)
    if split:
        array = array * block_levels(rng, dims, split, -0.22, 0.18)
    return jnp.clip(array, -reach, reach).astype(held_as)


def setup_inputs(seed: int = 0) -> dict:
    keys = jax.random.split(jax.random.key(seed), 7)
    inputs = normal_values(keys[0], (TOKENS, D), 1.0, 6.0, ((0, 32), (1, 8)))
    kv_grads = normal_values(keys[1], (TOKENS, KV), 1.0, 6.0, ((0, 32), (1, 2)))
    weight = normal_values(keys[2], (D, KV), KV ** -0.5, 0.25, ((0, 8), (1, 2)))
    master = normal_values(keys[3], (N_MROW, N_DP, SHARD, KV), 1.0, 6.0, ((0, 8), (1, 32), (3, 2)), jnp.float32)
    row_state = draw_row_state(jax.random.fold_in(keys[6], 71), 0)
    col_state = draw_col_state(jax.random.fold_in(keys[6], 71), 0)
    return {"inputs": inputs, "kv_grads": kv_grads, "weight": weight, "master": master, "row_state": row_state, "col_state": col_state}


def factored_step(g, p, rows, cols):
    sq = g * g + 1e-30
    row_new = 0.8 * rows + 0.2 * lax.optimization_barrier(jnp.mean(sq, axis=1))
    col_new = 0.8 * cols + 0.2 * lax.optimization_barrier(jnp.sum(sq, axis=0)) / D
    row_avg = jnp.sum(row_new) / D
    second = row_new[:, None] * col_new[None, :] / row_avg
    update = g / jnp.sqrt(second)
    update_rms = jnp.sqrt(jnp.sum(update * update) / (D * HEAD))
    param_rms = jnp.sqrt(jnp.sum(p * p) / (D * HEAD))
    clip = jnp.maximum(jnp.float32(1.0), update_rms)
    return (p - 0.5 * param_rms * update / clip, row_new, col_new)

def reference(inputs, kv_grads, weight, master, row_state, col_state):
    grad = jnp.dot(inputs.T, kv_grads, preferred_element_type=jnp.float32)
    params = master.reshape(D, KV)
    rows = row_state.reshape(2, D)
    new_p = []
    new_r = []
    new_c = []
    for which in range(2):
        lo = which * HEAD
        p_new, r_new, c_new = factored_step(grad[:, lo:lo + HEAD], params[:, lo:lo + HEAD], rows[which], col_state[which])
        new_p.append(p_new)
        new_r.append(r_new)
        new_c.append(c_new)
    new_params = jnp.concatenate(new_p, axis=1)
    new_master = new_params.reshape(N_MROW, N_DP, SHARD, KV)
    new_rows = jnp.stack(new_r).reshape(2, N_MROW, N_DP, SHARD)
    new_cols = jnp.stack(new_c)
    new_weight = new_params.astype(jnp.bfloat16)
    key_part = jnp.dot(kv_grads[:, :HEAD], weight[:, :HEAD].T, preferred_element_type=jnp.float32).astype(jnp.bfloat16)
    value_part = jnp.dot(kv_grads[:, HEAD:], weight[:, HEAD:].T, preferred_element_type=jnp.float32).astype(jnp.bfloat16)
    input_grad = (key_part.astype(jnp.float32) + value_part.astype(jnp.float32)).astype(jnp.bfloat16)
    return (new_master, new_rows, new_cols, new_weight, input_grad)
```

```python
import jax
import jax.numpy as jnp
from jax import lax
from jax.experimental import pallas as pl
from jax.experimental.pallas import tpu as pltpu
from jax.sharding import PartitionSpec as P

D = 8192
HEAD = 256
MESH = pl.DeviceIdType.MESH
BF = jnp.bfloat16
F32 = jnp.float32

AGG = (-6, 6, -3, 3, 0)
FAR = AGG[:4]
NEAR = ((1, 1), (-1, 1), (1, 0), (-1, 0), (0, 1))
FAR_SIDE = ((2, 1), (2, 0))
XY = tuple((y, h, l) for y in range(4) for h in range(2) for l in range(2) if (y, h, l) != (0, 0, 0))
ZS = tuple(range(1, 16))
B = 32


def kernel(a_hbm, kv_hbm, w_hbm, m_ref, r_ref, c_ref,
           nm_ref, nr_ref, nc_ref, nw_ref, ig_hbm,
           a_v, kv, kvo, w_v, wo, ig_v, grad, s1_out, s1_in, s1_far, s2_out, s2_in,
           hbuf, pbuf, pnear, pfar, st1, st2,
           loc, core_s, core_r, a_s, a_r, b_s, b_r, c_s, c_r, d_s, d_r,
           p_s, p_r, q_s, q_r, x_s, x_r, z_s, z_r):
    dp = lax.axis_index("dp")
    mrow = lax.axis_index("mrow")
    core = lax.axis_index("mcol")
    z, xh = dp // 2, dp % 2
    y, xl = mrow // 2, mrow % 2

    def dev(dz=0, dx=0, dy=0, dl=0, dc=0):
        return (
            ((z + dz + 16) % 16) * 2 + (xh + dx) % 2,
            ((y + dy + 4) % 4) * 2 + (xl + dl) % 2,
            (core + dc) % 2,
        )

    def block(dz, dx):
        return ((z + dz + 32) % 16) * 2 + (xh + dx) % 2

    def rows(index):
        return pl.ds(pl.multiple_of(index * B, B), B)

    def send(src, dst, ssem, rsem, to):
        copy = pltpu.make_async_remote_copy(
            src_ref=src, dst_ref=dst, send_sem=ssem, recv_sem=rsem, device_id=to, device_id_type=MESH
        )
        copy.start()
        return copy

    def arrived(dst, ssem, rsem):
        pltpu.make_async_remote_copy(
            src_ref=dst, dst_ref=dst, send_sem=ssem, recv_sem=rsem, device_id=dev(dc=1), device_id_type=MESH
        ).wait_recv()

    load_kv = pltpu.make_async_copy(kv_hbm, kv, loc.at[0])
    load_a = pltpu.make_async_copy(a_hbm, a_v, loc.at[1])
    load_w = pltpu.make_async_copy(w_hbm, w_v, loc.at[2])
    load_kv.start()
    load_a.start()
    load_w.start()

    peers = [dev(dz=d) for d in ZS]
    peers += [dev(dy=py, dx=ph, dl=pl_) for py, ph, pl_ in XY]
    peers += [dev(dz=d, dx=1) for d in (1, -1, 2, -2)]
    peers += [dev(dc=1)]
    barrier = pltpu.get_barrier_semaphore()
    for to in peers:
        pl.semaphore_signal(barrier, inc=1, device_id=to, device_id_type=MESH)

    load_kv.wait()
    load_a.wait()

    def grad_step(i, _):
        cols = pl.ds(pl.multiple_of(i * 256, 256), 256)
        grad[cols, :] = lax.dot_general(
            a_v[:, cols], kv[...], (((0,), (0,)), ((), ())), preferred_element_type=F32
        )
        return 0

    lax.fori_loop(0, 4, grad_step, 0)
    for n, (o, x) in enumerate(NEAR):
        for j, a in enumerate(AGG):
            s1_out[n, j * B:(j + 1) * B, :] = grad[rows(block(o - a, x)), :].astype(BF)
    for n, (o, x) in enumerate(FAR_SIDE):
        s1_out[5 + n, 0:B, :] = grad[rows(block(-o - 6, x)), :].astype(BF)

    load_w.wait()
    pl.semaphore_wait(barrier, len(peers))

    sent = []
    for n, (o, x) in enumerate(NEAR):
        sent.append(send(s1_out.at[n], s1_in.at[n], a_s.at[n], a_r.at[n], dev(dz=o, dx=x)))
    for n, (o, x) in enumerate(FAR_SIDE):
        sent.append(send(s1_out.at[5 + n, pl.ds(0, B)], s1_far.at[n], a_s.at[5 + n], a_r.at[5 + n], dev(dz=-o, dx=x)))

    half = w_v.shape[0] // 2
    mine = pl.ds(pl.multiple_of(core * half, half), half)
    theirs = pl.ds(pl.multiple_of((1 - core) * half, half), half)
    sent.append(send(kv, kvo, core_s.at[0], core_r.at[0], dev(dc=1)))
    sent.append(send(w_v.at[theirs], wo, core_s.at[1], core_r.at[1], dev(dc=1)))

    params = m_ref[0, 0]
    pbuf[4] = params.astype(BF)
    for j, a in enumerate(FAR):
        sent.append(send(pbuf.at[4], pbuf.at[j], p_s.at[j], p_r.at[j], dev(dz=a)))

    arrived(kvo, core_s.at[0], core_r.at[0])
    arrived(wo, core_s.at[1], core_r.at[1])

    def ig_step(i, _):
        toks = pl.ds(pl.multiple_of(i * 256, 256), 256)
        dims = (((1,), (1,)), ((), ()))
        own = lax.dot_general(kv[toks, :], w_v[mine, :], dims, preferred_element_type=F32).astype(BF)
        other = lax.dot_general(kvo[toks, :], wo[...], dims, preferred_element_type=F32).astype(BF)
        ig_v[toks, :] = (own.astype(F32) + other.astype(F32)).astype(BF)
        return 0

    lax.fori_loop(0, 4, ig_step, 0)
    store_ig = pltpu.make_async_copy(ig_v, ig_hbm, loc.at[3])
    store_ig.start()

    for n in range(5):
        arrived(s1_in.at[n], a_s.at[n], a_r.at[n])
    for n in range(2):
        arrived(s1_far.at[n], a_s.at[5 + n], a_r.at[5 + n])
    total = None
    for j, a in enumerate(AGG):
        part = grad[rows(block(-a, 0)), :]
        for n in range(5):
            part = part + s1_in[n, j * B:(j + 1) * B, :].astype(F32)
        if a == 6:
            for n in range(2):
                part = part + s1_far[n].astype(F32)
        if a == 0:
            total = part
        else:
            s2_out[j] = part.astype(BF)
            sent.append(send(s2_out.at[j], s2_in.at[j], b_s.at[j], b_r.at[j], dev(dz=-a)))

    for j in range(4):
        arrived(pbuf.at[j], p_s.at[j], p_r.at[j])
    for n, (o, x) in enumerate(NEAR):
        sent.append(send(pbuf, pnear.at[n], q_s.at[n], q_r.at[n], dev(dz=o, dx=x)))
    for n, (o, x) in enumerate(FAR_SIDE):
        sent.append(send(pbuf.at[1], pfar.at[n], q_s.at[5 + n], q_r.at[5 + n], dev(dz=o, dx=x)))

    for j in range(4):
        arrived(s2_in.at[j], b_s.at[j], b_r.at[j])
        total = total + s2_in[j].astype(F32)
    g = total

    eye = (lax.broadcasted_iota(jnp.int32, (B, B), 0) == lax.broadcasted_iota(jnp.int32, (B, B), 1)).astype(F32)
    old_rows = jnp.sum(eye * r_ref[0, 0], axis=1, keepdims=True)
    sq = g * g + 1e-30
    new_rows = 0.8 * old_rows + 0.2 * (jnp.sum(sq, axis=1, keepdims=True) * (1.0 / HEAD))
    h = g / jnp.sqrt(new_rows)
    hbuf[rows(dp), :] = h.astype(BF)
    col = jnp.sum(sq, axis=0, keepdims=True)
    weighted = jnp.sum(h * h, axis=0, keepdims=True)
    my_xy = y * 4 + xh * 2 + xl
    one = jnp.ones((1, 128), F32)
    st1[my_xy] = jnp.concatenate(
        [col[:, :128], col[:, 128:], weighted[:, :128], weighted[:, 128:],
         one * jnp.sum(new_rows), one * jnp.sum(params * params), one, one], axis=0)
    for n, (py, ph, pl_) in enumerate(XY):
        sent.append(send(st1.at[my_xy], st1.at[my_xy], x_s.at[n], x_r.at[n], dev(dy=py, dx=ph, dl=pl_)))

    for j, a in enumerate(FAR):
        sent.append(send(hbuf.at[rows(dp)], hbuf.at[rows(dp)], c_s.at[j], c_r.at[j], dev(dz=a)))

    def forward(j):
        a = AGG[j]
        src = hbuf.at[rows(block(-a, 0))]
        for n, (o, x) in enumerate(NEAR):
            sent.append(send(src, src, d_s.at[j, n], d_r.at[j, n], dev(dz=o, dx=x)))
        if a == 6:
            for n, (o, x) in enumerate(FAR_SIDE):
                sent.append(send(src, src, d_s.at[5, n], d_r.at[5, n], dev(dz=o, dx=x)))

    forward(4)
    nr_ref[0, 0] = jnp.sum(eye * new_rows, axis=0, keepdims=True)
    for j in (2, 3):
        arrived(hbuf.at[rows(block(-AGG[j], 0))], c_s.at[j], c_r.at[j])
        forward(j)
    for n, (py, ph, pl_) in enumerate(XY):
        src = ((y - py + 4) % 4) * 4 + ((xh + ph) % 2) * 2 + (xl + pl_) % 2
        arrived(st1.at[src], x_s.at[n], x_r.at[n])
    plane = st1[0]
    for i in range(1, 16):
        plane = plane + st1[i]
    st2[z] = plane
    for n, d in enumerate(ZS):
        sent.append(send(st2.at[z], st2.at[z], z_s.at[n], z_r.at[n], dev(dz=d)))
    for j in (0, 1):
        arrived(hbuf.at[rows(block(-AGG[j], 0))], c_s.at[j], c_r.at[j])
        forward(j)
    for n, (o, x) in enumerate(NEAR):
        arrived(pnear.at[n], q_s.at[n], q_r.at[n])
    for n in range(2):
        arrived(pfar.at[n], q_s.at[5 + n], q_r.at[5 + n])
    for n, d in enumerate(ZS):
        arrived(st2.at[(z - d + 16) % 16], z_s.at[n], z_r.at[n])
    whole = st2[0]
    for i in range(1, 16):
        whole = whole + st2[i]
    col_sum = jnp.concatenate([whole[0:1], whole[1:2]], axis=1)
    weight_sum = jnp.concatenate([whole[2:3], whole[3:4]], axis=1)
    row_avg = whole[4:5, 0:1] / D
    param_rms = jnp.sqrt(whole[5:6, 0:1] / (D * HEAD))
    new_cols = 0.8 * c_ref[...] + 0.2 * col_sum / D
    nc_ref[...] = new_cols
    update_sq = row_avg * jnp.sum(weight_sum / new_cols, axis=1, keepdims=True)
    clip = jnp.maximum(1.0, jnp.sqrt(update_sq / (D * HEAD)))
    scale = (0.5 * param_rms / clip) * (jnp.sqrt(row_avg) / jnp.sqrt(new_cols))
    nm_ref[0, 0] = params - h * scale

    for j in range(5):
        for n, (o, x) in enumerate(NEAR):
            arrived(hbuf.at[rows(block(-o - AGG[j], x))], d_s.at[j, n], d_r.at[j, n])
    for n, (o, x) in enumerate(FAR_SIDE):
        arrived(hbuf.at[rows(block(-o - 6, x))], d_s.at[5, n], d_r.at[5, n])

    def finish(p, index):
        nw_ref[rows(index), :] = (p.astype(F32) - hbuf[rows(index), :].astype(F32) * scale).astype(BF)

    for j, a in enumerate(AGG):
        finish(pbuf[j], block(-a, 0))
        for n, (o, x) in enumerate(NEAR):
            finish(pnear[n, j], block(-o - a, x))
    for n, (o, x) in enumerate(FAR_SIDE):
        finish(pfar[n], block(-o - 6, x))

    for copy in sent:
        copy.wait_send()
    store_ig.wait()


def on_device(inputs, kv_grads, weight, master, row_state, col_state):
    vmem = pl.BlockSpec(memory_space=pltpu.VMEM)
    hbm = pl.BlockSpec(memory_space=pl.ANY)
    dma = pltpu.SemaphoreType.DMA
    return pl.pallas_call(
        kernel,
        out_shape=(
            jax.ShapeDtypeStruct((1, 1, 32, 256), F32),
            jax.ShapeDtypeStruct((1, 1, 1, 32), F32),
            jax.ShapeDtypeStruct((1, 256), F32),
            jax.ShapeDtypeStruct((1024, 256), BF),
            jax.ShapeDtypeStruct((1024, 512), BF),
        ),
        in_specs=[hbm, hbm, hbm, vmem, vmem, vmem],
        out_specs=(vmem, vmem, vmem, vmem, hbm),
        scratch_shapes=[
            pltpu.VMEM((1024, 1024), BF),
            pltpu.VMEM((1024, 256), BF),
            pltpu.VMEM((1024, 256), BF),
            pltpu.VMEM((1024, 256), BF),
            pltpu.VMEM((512, 256), BF),
            pltpu.VMEM((1024, 512), BF),
            pltpu.VMEM((1024, 256), F32),
            pltpu.VMEM((7, 5 * B, 256), BF),
            pltpu.VMEM((5, 5 * B, 256), BF),
            pltpu.VMEM((2, B, 256), BF),
            pltpu.VMEM((4, B, 256), BF),
            pltpu.VMEM((4, B, 256), BF),
            pltpu.VMEM((1024, 256), BF),
            pltpu.VMEM((5, B, 256), BF),
            pltpu.VMEM((5, 5, B, 256), BF),
            pltpu.VMEM((2, B, 256), BF),
            pltpu.VMEM((16, 8, 128), F32),
            pltpu.VMEM((16, 8, 128), F32),
            dma((4,)), dma((2,)), dma((2,)), dma((7,)), dma((7,)), dma((4,)), dma((4,)),
            dma((4,)), dma((4,)), dma((6, 5)), dma((6, 5)), dma((4,)), dma((4,)),
            dma((7,)), dma((7,)), dma((15,)), dma((15,)), dma((15,)), dma((15,)),
        ],
        compiler_params=pltpu.CompilerParams(
            collective_id=0, has_side_effects=True, vmem_limit_bytes=40 << 20
        ),
        name="kv_backward_adafactor",
    )(inputs, kv_grads, weight, master, row_state, col_state)


def solution(mesh):
    placed = (
        P("dp", "mrow"),
        P("dp", "mcol"),
        P("mrow", "mcol"),
        P("mrow", "dp", None, "mcol"),
        P("mcol", "mrow", "dp", None),
        P("mcol", None),
    )
    return jax.shard_map(
        on_device,
        mesh=mesh,
        in_specs=placed,
        out_specs=(
            P("mrow", "dp", None, "mcol"),
            P("mcol", "mrow", "dp", None),
            P("mcol", None),
            P("mrow", "mcol"),
            P("dp", ("mrow", "mcol")),
        ),
        check_vma=False,
    )
```

```python
import jax
import jax.numpy as jnp
from jax import lax
from jax.experimental import pallas as pl
from jax.experimental.pallas import tpu as pltpu
from jax.sharding import PartitionSpec as P

D = 8192
HEAD = 256
MESH = pl.DeviceIdType.MESH
BF = jnp.bfloat16
F32 = jnp.float32

AGG = (-6, 6, -3, 3, 0)
FAR = AGG[:4]
NEAR = ((1, 1), (-1, 1), (1, 0), (-1, 0), (0, 1))
SIDE = ((2, 1), (2, 0))
XY = ((2, 1, 1), (1, 1, 1), (3, 1, 1), (2, 1, 0), (2, 0, 1), (1, 1, 0), (3, 1, 0), (0, 1, 1),
      (2, 0, 0), (1, 0, 1), (3, 0, 1), (0, 1, 0), (1, 0, 0), (3, 0, 0), (0, 0, 1))
ZS = (8, 7, 9, 6, 10, 5, 11, 4, 12, 3, 13, 2, 14, 1, 15)
B = 32


def kernel(a_hbm, kv_hbm, w_hbm, m_hbm, r_hbm, c_hbm,
           nm_ref, nr_ref, nc_ref, nw_ref, ig_ref,
           m_ref, r_ref, c_ref, a_v, kv, kvo, w_v, wo, grad,
           f_out, f_in, n_out, n_in, side_out, side_in, s2_out, s2_in,
           hbuf, pbuf, pz, pfar, st1, st2, loc, core_s, core_r,
           f_s, f_r, n_s, n_r, side_s, side_r, b_s, b_r, c_s, c_r, d_s, d_r, e_s, e_r,
           p_s, p_r, px_s, px_r, q_s, q_r, qf_s, qf_r, x_s, x_r, z_s, z_r, known3, known6, plane1, plane2):
    dp = lax.axis_index("dp")
    mrow = lax.axis_index("mrow")
    core = lax.axis_index("mcol")
    z, xh = lax.div(dp, 2), lax.rem(dp, 2)
    y, xl = lax.div(mrow, 2), lax.rem(mrow, 2)
    at_x = (xh, 1 - xh)
    at_l = (xl, 1 - xl)
    at_z = [z] + [lax.rem(z + d, 16) for d in range(1, 16)]
    at_y = [y] + [lax.rem(y + d, 4) for d in range(1, 4)]
    at_dp = [[at_z[d] * 2 + at_x[x] for x in range(2)] for d in range(16)]
    at_mrow = [[at_y[d] * 2 + at_l[l] for l in range(2)] for d in range(4)]
    at_core = (core, 1 - core)
    at_rows = [[pl.multiple_of(at_dp[d][x] * B, B) for x in range(2)] for d in range(16)]

    def dev(dz=0, dx=0, dy=0, dl=0, dc=0):
        return at_dp[dz % 16][dx], at_mrow[dy % 4][dl], at_core[dc]

    def rows(dz, dx):
        return pl.ds(at_rows[dz % 16][dx], B)

    sent, pending = [], {}

    def send(src, dst, sems, n, to):
        copy = pltpu.make_async_remote_copy(
            src_ref=src, dst_ref=dst, send_sem=sems[0].at[n], recv_sem=sems[1].at[n],
            device_id=to, device_id_type=MESH,
        )
        copy.start()
        sent.append(copy)
        pending[id(sems[1]), n] = copy

    def arrived(dst, sems, n):
        pltpu.make_async_remote_copy(
            src_ref=dst, dst_ref=dst, send_sem=sems[0].at[n], recv_sem=sems[1].at[n],
            device_id=dev(dc=1), device_id_type=MESH,
        ).wait_recv()
        del pending[id(sems[1]), n]

    loads = [
        pltpu.make_async_copy(src, dst, loc.at[i])
        for i, (src, dst) in enumerate(
            ((kv_hbm, kv), (w_hbm, w_v), (m_hbm, m_ref), (r_hbm, r_ref), (c_hbm, c_ref)))
    ]
    chunks = [pl.ds(i * 256, 256) for i in range(4)]
    loads_a = [pltpu.make_async_copy(a_hbm.at[:, c], a_v.at[:, c], loc.at[5 + i]) for i, c in enumerate(chunks)]
    loads[0].start()
    for copy in loads_a + loads[1:]:
        copy.start()

    peers = [dev(dz=d, dx=x) for d in (1, -1, 2, -2) for x in (0, 1)]
    peers += [dev(dz=d) for d in (3, -3)]
    peers += [dev(dx=1), dev(dy=1), dev(dy=-1), dev(dl=1), dev(dc=1)]
    barrier = pltpu.get_barrier_semaphore()
    for to in peers:
        pl.semaphore_signal(barrier, inc=1, device_id=to, device_id_type=MESH)

    loads[0].wait()
    for copy, c in zip(loads_a, chunks):
        copy.wait()
        grad[c, :] = lax.dot_general(
            a_v[:, c], kv[...], (((0,), (0,)), ((), ())), preferred_element_type=F32
        )
    for n, (o, x) in enumerate(SIDE):
        side_out[n] = grad[rows(-o - 6, x), :].astype(BF)
    for n, (o, x) in enumerate(NEAR):
        for j in range(2):
            f_out[n, j * B:(j + 1) * B, :] = grad[rows(o - AGG[j], x), :].astype(BF)
        for j in range(3):
            n_out[n, j * B:(j + 1) * B, :] = grad[rows(o - AGG[2 + j], x), :].astype(BF)

    for copy in loads[1:]:
        copy.wait()
    pl.semaphore_wait(barrier, len(peers))

    for n, (o, x) in enumerate(SIDE):
        send(side_out.at[n], side_in.at[n], (side_s, side_r), n, dev(dz=-o, dx=x))
    for n, (o, x) in enumerate(NEAR):
        send(f_out.at[n], f_in.at[n], (f_s, f_r), n, dev(dz=o, dx=x))
    for d in (3, -3):
        pl.semaphore_signal(known3, inc=1, device_id=dev(dz=d), device_id_type=MESH)
    for to in (dev(dy=1), dev(dy=-1), dev(dl=1), dev(dx=1)):
        pl.semaphore_signal(plane1, inc=1, device_id=to, device_id_type=MESH)
    for n, (o, x) in enumerate(NEAR):
        send(n_out.at[n], n_in.at[n], (n_s, n_r), n, dev(dz=o, dx=x))

    params = m_ref[0, 0]
    pbuf[4] = params.astype(BF)
    for j in (2, 3):
        send(pbuf.at[4], pbuf.at[j], (p_s, p_r), j, dev(dz=AGG[j]))
    pl.semaphore_wait(known3, 2)
    for d in (6, -6):
        pl.semaphore_signal(known6, inc=1, device_id=dev(dz=d), device_id_type=MESH)
    for j in (0, 1):
        send(pbuf.at[4], pbuf.at[j], (p_s, p_r), j, dev(dz=AGG[j]))
    pl.semaphore_wait(plane1, 4)
    for d in (1, -1, 2):
        pl.semaphore_signal(plane2, inc=1, device_id=dev(dy=d), device_id_type=MESH)
    half = w_v.shape[0] // 2
    mine = pl.ds(pl.multiple_of(core * half, half), half)
    theirs = pl.ds(pl.multiple_of((1 - core) * half, half), half)
    send(kv, kvo, (core_s, core_r), 0, dev(dc=1))
    send(w_v.at[theirs], wo, (core_s, core_r), 1, dev(dc=1))

    def aggregate(j):
        a = AGG[j]
        part = grad[rows(-a, 0), :]
        for n in range(5):
            got = f_in[n, j * B:(j + 1) * B, :] if j < 2 else n_in[n, (j - 2) * B:(j - 1) * B, :]
            part = part + got.astype(F32)
        if a == 6:
            for n in range(2):
                part = part + side_in[n].astype(F32)
        if a == 0:
            return part
        s2_out[j] = part.astype(BF)
        send(s2_out.at[j], s2_in.at[j], (b_s, b_r), j, dev(dz=-a))

    for n in range(2):
        arrived(side_in.at[n], (side_s, side_r), n)
    for n in range(5):
        arrived(f_in.at[n], (f_s, f_r), n)
    aggregate(0)
    aggregate(1)
    for n in range(5):
        arrived(n_in.at[n], (n_s, n_r), n)
    aggregate(2)
    aggregate(3)
    total = aggregate(4)

    for j in range(4):
        arrived(pbuf.at[j], (p_s, p_r), j)
    send(pbuf.at[pl.ds(0, 5)], pbuf.at[pl.ds(5, 5)], (px_s, px_r), 0, dev(dx=1))

    arrived(kvo, (core_s, core_r), 0)
    arrived(wo, (core_s, core_r), 1)

    def ig_step(i, _):
        toks = pl.ds(pl.multiple_of(i * 256, 256), 256)
        dims = (((1,), (1,)), ((), ()))
        own = lax.dot_general(kv[toks, :], w_v[mine, :], dims, preferred_element_type=F32).astype(BF)
        other = lax.dot_general(kvo[toks, :], wo[...], dims, preferred_element_type=F32).astype(BF)
        ig_ref[toks, :] = (own.astype(F32) + other.astype(F32)).astype(BF)
        return 0

    lax.fori_loop(0, 4, ig_step, 0)
    for copy in sent:
        copy.wait_send()
    sent.clear()
    for j in (2, 3, 0, 1):
        arrived(s2_in.at[j], (b_s, b_r), j)
        total = total + s2_in[j].astype(F32)
    g = total

    eye = (lax.broadcasted_iota(jnp.int32, (B, B), 0) == lax.broadcasted_iota(jnp.int32, (B, B), 1)).astype(F32)
    old_rows = jnp.sum(eye * r_ref[0, 0], axis=1, keepdims=True)
    sq = g * g + 1e-30
    new_rows = 0.8 * old_rows + 0.2 * (jnp.sum(sq, axis=1, keepdims=True) * (1.0 / HEAD))
    h = g / jnp.sqrt(new_rows)
    hbuf[rows(0, 0), :] = h.astype(BF)
    col = jnp.sum(sq, axis=0, keepdims=True)
    weighted = jnp.sum(h * h, axis=0, keepdims=True)
    pl.semaphore_wait(plane2, 3)
    my_xy = y * 4 + xh * 2 + xl
    left = lax.broadcasted_iota(jnp.int32, (1, 128), 1) < 64
    st1[my_xy] = jnp.concatenate(
        [col[:, :128], col[:, 128:], weighted[:, :128], weighted[:, 128:],
         jnp.where(left, jnp.sum(new_rows), jnp.sum(params * params))], axis=0)
    for n, (py, ph, pl_) in enumerate(XY):
        send(st1.at[my_xy], st1.at[my_xy], (x_s, x_r), n, dev(dy=py, dx=ph, dl=pl_))

    for j, a in enumerate(FAR):
        send(hbuf.at[rows(0, 0)], hbuf.at[rows(0, 0)], (c_s, c_r), j, dev(dz=a))

    def forward(j):
        src = hbuf.at[rows(-AGG[j], 0)]
        for n, (o, x) in enumerate(NEAR):
            send(src, src, (d_s, d_r), j * 5 + n, dev(dz=o, dx=x))
        if AGG[j] == 6:
            for n, (o, x) in enumerate(SIDE):
                send(src, src, (e_s, e_r), n, dev(dz=o, dx=x))

    forward(4)
    arrived(pbuf.at[pl.ds(5, 5)], (px_s, px_r), 0)
    for n in range(2):
        send(pbuf.at[5 * n + 1], pfar.at[n], (qf_s, qf_r), n, dev(dz=2))
    for n, o in enumerate((1, -1)):
        send(pbuf, pz.at[n], (q_s, q_r), n, dev(dz=o))
    nr_ref[0, 0] = jnp.sum(eye * new_rows, axis=0, keepdims=True)
    pl.semaphore_wait(known6, 2)
    for j in (2, 3):
        arrived(hbuf.at[rows(-AGG[j], 0)], (c_s, c_r), j)
        forward(j)
    for n, (py, ph, pl_) in enumerate(XY):
        src = at_y[-py % 4] * 4 + at_x[ph] * 2 + at_l[pl_]
        arrived(st1.at[src], (x_s, x_r), n)
    plane = st1[0]
    for i in range(1, 16):
        plane = plane + st1[i]
    st2[z] = plane
    early = len(sent)
    for n, d in enumerate(ZS):
        send(st2.at[z], st2.at[z], (z_s, z_r), n, dev(dz=d))
    for j in (0, 1):
        arrived(hbuf.at[rows(-AGG[j], 0)], (c_s, c_r), j)
        forward(j)

    for copy in sent[:early]:
        copy.wait_send()
    del sent[:early]
    for j in (4, 2, 3):
        for n, (o, x) in enumerate(NEAR):
            arrived(hbuf.at[rows(-o - AGG[j], x)], (d_s, d_r), j * 5 + n)
    for n, d in enumerate(ZS):
        arrived(st2.at[at_z[-d % 16]], (z_s, z_r), n)
    whole = st2[0]
    for i in range(1, 16):
        whole = whole + st2[i]
    col_sum = jnp.concatenate([whole[0:1], whole[1:2]], axis=1)
    weight_sum = jnp.concatenate([whole[2:3], whole[3:4]], axis=1)
    row_avg = whole[4:5, 0:1] / D
    param_rms = jnp.sqrt(whole[4:5, 64:65] / (D * HEAD))
    new_cols = 0.8 * c_ref[...] + 0.2 * col_sum / D
    nc_ref[...] = new_cols
    update_sq = row_avg * jnp.sum(weight_sum / new_cols, axis=1, keepdims=True)
    clip = jnp.maximum(1.0, jnp.sqrt(update_sq / (D * HEAD)))
    scale = (0.5 * param_rms / clip) * (jnp.sqrt(row_avg) / jnp.sqrt(new_cols))
    nm_ref[0, 0] = params - h * scale

    for j in range(2):
        for n, (o, x) in enumerate(NEAR):
            arrived(hbuf.at[rows(-o - AGG[j], x)], (d_s, d_r), j * 5 + n)
    for n, (o, x) in enumerate(SIDE):
        arrived(hbuf.at[rows(-o - 6, x)], (e_s, e_r), n)
    for n, o in enumerate((1, -1)):
        arrived(pz.at[n], (q_s, q_r), n)
    for n in range(2):
        arrived(pfar.at[n], (qf_s, qf_r), n)

    def finish(p, index):
        nw_ref[index, :] = (p.astype(F32) - hbuf[index, :].astype(F32) * scale).astype(BF)

    for x in range(2):
        for j, a in enumerate(AGG):
            finish(pbuf[5 * x + j], rows(-a, x))
            for n, o in enumerate((1, -1)):
                finish(pz[n, 5 * x + j], rows(-o - a, x))
        finish(pfar[x], rows(-8, x))

    for copy in sent:
        copy.wait_send()


def hand_over(*refs):
    n = len(refs) // 2
    sems = refs[-1]
    copies = [pltpu.make_async_copy(refs[i], refs[n + i], sems.at[i]) for i in range(n)]
    for copy in copies:
        copy.start()
    for copy in copies:
        copy.wait()


def on_device(inputs, kv_grads, weight, master, row_state, col_state):
    hbm = pl.BlockSpec(memory_space=pltpu.HBM)
    anywhere = pl.BlockSpec(memory_space=pl.ANY)
    vmem = pl.BlockSpec(memory_space=pltpu.VMEM)
    dma = pltpu.SemaphoreType.DMA
    out_shape = (
        jax.ShapeDtypeStruct((1, 1, 32, 256), F32),
        jax.ShapeDtypeStruct((1, 1, 1, 32), F32),
        jax.ShapeDtypeStruct((1, 256), F32),
        jax.ShapeDtypeStruct((1024, 256), BF),
        jax.ShapeDtypeStruct((1024, 512), BF),
    )
    results = pl.pallas_call(
        kernel,
        out_shape=out_shape,
        in_specs=[hbm] * 6,
        out_specs=(vmem,) * 5,
        scratch_shapes=[
            pltpu.VMEM((1, 1, 32, 256), F32),
            pltpu.VMEM((1, 1, 1, 32), F32),
            pltpu.VMEM((1, 256), F32),
            pltpu.VMEM((1024, 1024), BF),
            pltpu.VMEM((1024, 256), BF),
            pltpu.VMEM((1024, 256), BF),
            pltpu.VMEM((1024, 256), BF),
            pltpu.VMEM((512, 256), BF),
            pltpu.VMEM((1024, 256), F32),
            pltpu.VMEM((5, 2 * B, 256), BF),
            pltpu.VMEM((5, 2 * B, 256), BF),
            pltpu.VMEM((5, 3 * B, 256), BF),
            pltpu.VMEM((5, 3 * B, 256), BF),
            pltpu.VMEM((2, B, 256), BF),
            pltpu.VMEM((2, B, 256), BF),
            pltpu.VMEM((4, B, 256), BF),
            pltpu.VMEM((4, B, 256), BF),
            pltpu.VMEM((1024, 256), BF),
            pltpu.VMEM((10, B, 256), BF),
            pltpu.VMEM((2, 10, B, 256), BF),
            pltpu.VMEM((2, B, 256), BF),
            pltpu.VMEM((16, 5, 128), F32),
            pltpu.VMEM((16, 5, 128), F32),
            dma((9,)),
        ] + [dma((n,)) for n in (2, 5, 5, 2, 4, 4, 25, 2, 4, 1, 2, 2, 15, 15) for _ in range(2)] + [
            pltpu.SemaphoreType.REGULAR] + [pltpu.SemaphoreType.REGULAR] * 3,
        compiler_params=pltpu.CompilerParams(
            collective_id=0, has_side_effects=True, vmem_limit_bytes=24 << 20
        ),
        name="kv_backward_adafactor",
    )(*[pltpu.with_memory_space_constraint(x, pltpu.HBM) for x in (inputs, kv_grads, weight, master, row_state, col_state)])
    return pl.pallas_call(
        hand_over,
        out_shape=out_shape,
        in_specs=[anywhere] * 5,
        out_specs=(hbm,) * 5,
        scratch_shapes=[dma((5,))],
        compiler_params=pltpu.CompilerParams(vmem_limit_bytes=16 << 20),
        name="hand_over",
    )(*results)


def solution(mesh):
    placed = (
        P("dp", "mrow"),
        P("dp", "mcol"),
        P("mrow", "mcol"),
        P("mrow", "dp", None, "mcol"),
        P("mcol", "mrow", "dp", None),
        P("mcol", None),
    )
    return jax.shard_map(
        on_device,
        mesh=mesh,
        in_specs=placed,
        out_specs=(
            P("mrow", "dp", None, "mcol"),
            P("mcol", "mrow", "dp", None),
            P("mcol", None),
            P("mrow", "mcol"),
            P("dp", ("mrow", "mcol")),
        ),
        check_vma=False,
    )
```

```python
import jax
import jax.numpy as jnp
from jax import lax
from jax.experimental import pallas as pl
from jax.experimental.pallas import tpu as pltpu
from jax.sharding import PartitionSpec as P

D = 8192
HEAD = 256
MESH = pl.DeviceIdType.MESH
BF = jnp.bfloat16
F32 = jnp.float32

AGG = (-6, 6, -3, 3, 0)
FAR = AGG[:4]
NEAR = ((1, 1), (-1, 1), (1, 0), (-1, 0), (0, 1))
SIDE = ((2, 1), (2, 0))
XY = ((2, 1, 1), (1, 1, 1), (3, 1, 1), (2, 1, 0), (2, 0, 1), (1, 1, 0), (3, 1, 0), (0, 1, 1),
      (2, 0, 0), (1, 0, 1), (3, 0, 1), (0, 1, 0), (1, 0, 0), (3, 0, 0), (0, 0, 1))
ZS = (8, 7, 9, 6, 10, 5, 11, 4, 12, 3, 13, 2, 14, 1, 15)
B = 32


def kernel(a_hbm, kv_hbm, w_hbm, m_hbm, r_hbm, c_hbm,
           nm_ref, nr_ref, nc_ref, nw_ref, ig_ref,
           m_ref, r_ref, c_ref, a_v, kv, kvo, w_v, wo, grad,
           f_out, f_in, n_out, n_in, side_out, side_in, s2_out, s2_in,
           hbuf, pbuf, pz, pfar, st1, st2, loc, core_s, core_r,
           f_s, f_r, n_s, n_r, side_s, side_r, b_s, b_r, c_s, c_r, d_s, d_r, e_s, e_r,
           po_s, po_r, p_s, p_r, px_s, px_r, q_s, q_r, qf_s, qf_r, pb_s, pb_r, x_s, x_r, z_s, z_r, known3, known6, plane1, plane2):
    dp = lax.axis_index("dp")
    mrow = lax.axis_index("mrow")
    core = lax.axis_index("mcol")
    z, xh = lax.div(dp, 2), lax.rem(dp, 2)
    y, xl = lax.div(mrow, 2), lax.rem(mrow, 2)
    at_x = (xh, 1 - xh)
    at_l = (xl, 1 - xl)
    at_z = [z] + [lax.rem(z + d, 16) for d in range(1, 16)]
    at_y = [y] + [lax.rem(y + d, 4) for d in range(1, 4)]
    at_dp = [[at_z[d] * 2 + at_x[x] for x in range(2)] for d in range(16)]
    at_mrow = [[at_y[d] * 2 + at_l[l] for l in range(2)] for d in range(4)]
    at_core = (core, 1 - core)
    at_rows = [[pl.multiple_of(at_dp[d][x] * B, B) for x in range(2)] for d in range(16)]

    def dev(dz=0, dx=0, dy=0, dl=0, dc=0):
        return at_dp[dz % 16][dx], at_mrow[dy % 4][dl], at_core[dc]

    def rows(dz, dx):
        return pl.ds(at_rows[dz % 16][dx], B)

    sent = []

    def send(src, dst, sems, n, to, later=None):
        copy = pltpu.make_async_remote_copy(
            src_ref=src, dst_ref=dst, send_sem=sems[0].at[n], recv_sem=sems[1].at[n],
            device_id=to, device_id_type=MESH,
        )
        copy.start()
        if later is None:
            sent.append(copy)

    def left(src, sems, n):
        pltpu.make_async_remote_copy(
            src_ref=src, dst_ref=src, send_sem=sems[0].at[n], recv_sem=sems[1].at[n],
            device_id=dev(dc=1), device_id_type=MESH,
        ).wait_send()

    def arrived(dst, sems, n):
        pltpu.make_async_remote_copy(
            src_ref=dst, dst_ref=dst, send_sem=sems[0].at[n], recv_sem=sems[1].at[n],
            device_id=dev(dc=1), device_id_type=MESH,
        ).wait_recv()

    loads = [
        pltpu.make_async_copy(src, dst, loc.at[i])
        for i, (src, dst) in enumerate(
            ((kv_hbm, kv), (w_hbm, w_v), (m_hbm, m_ref), (r_hbm, r_ref), (c_hbm, c_ref)))
    ]
    chunks = [pl.ds(i * 256, 256) for i in range(4)]
    loads_a = [pltpu.make_async_copy(a_hbm.at[:, c], a_v.at[:, c], loc.at[5 + i]) for i, c in enumerate(chunks)]
    loads[0].start()
    for copy in loads_a + loads[1:]:
        copy.start()

    peers = [dev(dz=d, dx=x) for d in (1, -1, 2, -2) for x in (0, 1)]
    peers += [dev(dz=d) for d in (3, -3)]
    peers += [dev(dx=1), dev(dy=1), dev(dy=-1), dev(dl=1), dev(dc=1)]
    barrier = pltpu.get_barrier_semaphore()
    for to in peers:
        pl.semaphore_signal(barrier, inc=1, device_id=to, device_id_type=MESH)

    loads[0].wait()
    for copy, c in zip(loads_a, chunks):
        copy.wait()
        grad[c, :] = lax.dot_general(
            a_v[:, c], kv[...], (((0,), (0,)), ((), ())), preferred_element_type=F32
        )
    for n, (o, x) in enumerate(SIDE):
        side_out[n] = grad[rows(-o - 6, x), :].astype(BF)
    for n, (o, x) in enumerate(NEAR):
        for j in range(2):
            f_out[n, j * B:(j + 1) * B, :] = grad[rows(o - AGG[j], x), :].astype(BF)
        for j in range(3):
            n_out[n, j * B:(j + 1) * B, :] = grad[rows(o - AGG[2 + j], x), :].astype(BF)

    for copy in loads[1:]:
        copy.wait()
    pl.semaphore_wait(barrier, len(peers))

    for n, (o, x) in enumerate(SIDE):
        send(side_out.at[n], side_in.at[n], (side_s, side_r), n, dev(dz=-o, dx=x))
    for n, (o, x) in enumerate(NEAR):
        send(f_out.at[n], f_in.at[n], (f_s, f_r), n, dev(dz=o, dx=x))
    for d in (3, -3):
        pl.semaphore_signal(known3, inc=1, device_id=dev(dz=d), device_id_type=MESH)
    for to in (dev(dy=1), dev(dy=-1), dev(dl=1), dev(dx=1)):
        pl.semaphore_signal(plane1, inc=1, device_id=to, device_id_type=MESH)
    for n, (o, x) in enumerate(NEAR):
        send(n_out.at[n], n_in.at[n], (n_s, n_r), n, dev(dz=o, dx=x))

    params = m_ref[0, 0]
    pbuf[4, core] = params.astype(BF)

    @pl.when(core == 0)
    def _():
        send(pbuf.at[4, 0], pbuf.at[4, 0], (po_s, po_r), 0, dev(dc=1), ())
        left(pbuf.at[4, 0], (po_s, po_r), 0)

    pl.semaphore_wait(known3, 2)
    for d in (6, -6):
        pl.semaphore_signal(known6, inc=1, device_id=dev(dz=d), device_id_type=MESH)

    @pl.when(core == 1)
    def _():
        arrived(pbuf.at[4, 0], (po_s, po_r), 0)
        for j, a in enumerate(FAR):
            send(pbuf.at[4], pbuf.at[j], (p_s, p_r), j, dev(dz=a), ())

    pl.semaphore_wait(plane1, 4)
    for d in (1, -1, 2):
        pl.semaphore_signal(plane2, inc=1, device_id=dev(dy=d), device_id_type=MESH)
    half = w_v.shape[0] // 2
    mine = pl.ds(pl.multiple_of(core * half, half), half)
    theirs = pl.ds(pl.multiple_of((1 - core) * half, half), half)
    send(kv, kvo, (core_s, core_r), 0, dev(dc=1))
    send(w_v.at[theirs], wo, (core_s, core_r), 1, dev(dc=1))

    def aggregate(j):
        a = AGG[j]
        part = grad[rows(-a, 0), :]
        for n in range(5):
            got = f_in[n, j * B:(j + 1) * B, :] if j < 2 else n_in[n, (j - 2) * B:(j - 1) * B, :]
            part = part + got.astype(F32)
        if a == 6:
            for n in range(2):
                part = part + side_in[n].astype(F32)
        if a == 0:
            return part
        s2_out[j] = part.astype(BF)
        send(s2_out.at[j], s2_in.at[j], (b_s, b_r), j, dev(dz=-a))

    for n in range(2):
        arrived(side_in.at[n], (side_s, side_r), n)
    for n in range(5):
        arrived(f_in.at[n], (f_s, f_r), n)
    aggregate(0)
    aggregate(1)
    for n in range(5):
        arrived(n_in.at[n], (n_s, n_r), n)
    aggregate(2)
    aggregate(3)
    total = aggregate(4)

    @pl.when(core == 1)
    def _():
        for j in range(4):
            arrived(pbuf.at[j], (p_s, p_r), j)
        send(pbuf.at[pl.ds(0, 5)], pbuf.at[pl.ds(5, 5)], (px_s, px_r), 0, dev(dx=1), ())

    def third(x):
        if x == 1:
            arrived(pbuf.at[pl.ds(5, 5)], (px_s, px_r), 0)
        send(pbuf.at[5 * x + 1], pfar.at[x], (qf_s, qf_r), x, dev(dz=2), ())
        for n, o in enumerate((1, -1)):
            part = pl.ds(5 * x, 5)
            send(pbuf.at[part], pz.at[n, part], (q_s, q_r), 2 * n + x, dev(dz=o), ())

    @pl.when(core == 1)
    def _():
        third(0)

    arrived(kvo, (core_s, core_r), 0)
    arrived(wo, (core_s, core_r), 1)

    def ig_step(i, _):
        toks = pl.ds(pl.multiple_of(i * 256, 256), 256)
        dims = (((1,), (1,)), ((), ()))
        own = lax.dot_general(kv[toks, :], w_v[mine, :], dims, preferred_element_type=F32).astype(BF)
        other = lax.dot_general(kvo[toks, :], wo[...], dims, preferred_element_type=F32).astype(BF)
        ig_ref[toks, :] = (own.astype(F32) + other.astype(F32)).astype(BF)
        return 0

    lax.fori_loop(0, 4, ig_step, 0)
    for copy in sent:
        copy.wait_send()
    sent.clear()
    for j in (2, 3, 0, 1):
        arrived(s2_in.at[j], (b_s, b_r), j)
        total = total + s2_in[j].astype(F32)
    g = total

    eye = (lax.broadcasted_iota(jnp.int32, (B, B), 0) == lax.broadcasted_iota(jnp.int32, (B, B), 1)).astype(F32)
    old_rows = jnp.sum(eye * r_ref[0, 0], axis=1, keepdims=True)
    sq = g * g + 1e-30
    new_rows = 0.8 * old_rows + 0.2 * (jnp.sum(sq, axis=1, keepdims=True) * (1.0 / HEAD))
    h = g / jnp.sqrt(new_rows)
    hbuf[rows(0, 0), :] = h.astype(BF)
    col = jnp.sum(sq, axis=0, keepdims=True)
    weighted = jnp.sum(h * h, axis=0, keepdims=True)
    pl.semaphore_wait(plane2, 3)
    my_xy = y * 4 + xh * 2 + xl
    low = lax.broadcasted_iota(jnp.int32, (1, 128), 1) < 64
    st1[my_xy] = jnp.concatenate(
        [col[:, :128], col[:, 128:], weighted[:, :128], weighted[:, 128:],
         jnp.where(low, jnp.sum(new_rows), jnp.sum(params * params))], axis=0)
    for n, (py, ph, pl_) in enumerate(XY):
        send(st1.at[my_xy], st1.at[my_xy], (x_s, x_r), n, dev(dy=py, dx=ph, dl=pl_))

    for j, a in enumerate(FAR):
        send(hbuf.at[rows(0, 0)], hbuf.at[rows(0, 0)], (c_s, c_r), j, dev(dz=a))

    def forward(j):
        src = hbuf.at[rows(-AGG[j], 0)]
        for n, (o, x) in enumerate(NEAR):
            send(src, src, (d_s, d_r), j * 5 + n, dev(dz=o, dx=x))
        if AGG[j] == 6:
            for n, (o, x) in enumerate(SIDE):
                send(src, src, (e_s, e_r), n, dev(dz=o, dx=x))

    forward(4)
    @pl.when(core == 1)
    def _():
        third(1)

    nr_ref[0, 0] = jnp.sum(eye * new_rows, axis=0, keepdims=True)
    pl.semaphore_wait(known6, 2)
    for j in (2, 3):
        arrived(hbuf.at[rows(-AGG[j], 0)], (c_s, c_r), j)
        forward(j)
    for n, (py, ph, pl_) in enumerate(XY):
        src = at_y[-py % 4] * 4 + at_x[ph] * 2 + at_l[pl_]
        arrived(st1.at[src], (x_s, x_r), n)
    plane = st1[0]
    for i in range(1, 16):
        plane = plane + st1[i]
    st2[z] = plane
    early = len(sent)
    for n, d in enumerate(ZS):
        send(st2.at[z], st2.at[z], (z_s, z_r), n, dev(dz=d))
    for j in (0, 1):
        arrived(hbuf.at[rows(-AGG[j], 0)], (c_s, c_r), j)
        forward(j)

    for copy in sent[:early]:
        copy.wait_send()
    del sent[:early]
    @pl.when(core == 1)
    def _():
        for x in range(2):
            arrived(pfar.at[x], (qf_s, qf_r), x)
            for n in range(2):
                arrived(pz.at[n, pl.ds(5 * x, 5)], (q_s, q_r), 2 * n + x)
        for i, part in enumerate((pbuf.at[:, 0], pz.at[:, :, 0], pfar.at[:, 0])):
            send(part, part, (pb_s, pb_r), i, dev(dc=1), ())

    for j in (4, 2, 3):
        for n, (o, x) in enumerate(NEAR):
            arrived(hbuf.at[rows(-o - AGG[j], x)], (d_s, d_r), j * 5 + n)
    for n, d in enumerate(ZS):
        arrived(st2.at[at_z[-d % 16]], (z_s, z_r), n)
    whole = st2[0]
    for i in range(1, 16):
        whole = whole + st2[i]
    col_sum = jnp.concatenate([whole[0:1], whole[1:2]], axis=1)
    weight_sum = jnp.concatenate([whole[2:3], whole[3:4]], axis=1)
    row_avg = whole[4:5, 0:1] / D
    param_rms = jnp.sqrt(whole[4:5, 64:65] / (D * HEAD))
    new_cols = 0.8 * c_ref[...] + 0.2 * col_sum / D
    nc_ref[...] = new_cols
    update_sq = row_avg * jnp.sum(weight_sum / new_cols, axis=1, keepdims=True)
    clip = jnp.maximum(1.0, jnp.sqrt(update_sq / (D * HEAD)))
    scale = (0.5 * param_rms / clip) * (jnp.sqrt(row_avg) / jnp.sqrt(new_cols))
    nm_ref[0, 0] = params - h * scale

    for j in range(2):
        for n, (o, x) in enumerate(NEAR):
            arrived(hbuf.at[rows(-o - AGG[j], x)], (d_s, d_r), j * 5 + n)
    for n, (o, x) in enumerate(SIDE):
        arrived(hbuf.at[rows(-o - 6, x)], (e_s, e_r), n)
    for i in range(3):
        @pl.when(core == 0)
        def _():
            arrived((pbuf.at[:, 0], pz.at[:, :, 0], pfar.at[:, 0])[i], (pb_s, pb_r), i)

    def finish(p, index):
        nw_ref[index, :] = (p.astype(F32) - hbuf[index, :].astype(F32) * scale).astype(BF)

    for x in range(2):
        for j, a in enumerate(AGG):
            finish(pbuf[5 * x + j, core], rows(-a, x))
            for n, o in enumerate((1, -1)):
                finish(pz[n, 5 * x + j, core], rows(-o - a, x))
        finish(pfar[x, core], rows(-8, x))

    @pl.when(core == 1)
    def _():
        for j in range(4):
            left(pbuf.at[j], (p_s, p_r), j)
        left(pbuf.at[pl.ds(0, 5)], (px_s, px_r), 0)
        for x in range(2):
            left(pfar.at[x], (qf_s, qf_r), x)
            for n in range(2):
                left(pz.at[n, pl.ds(5 * x, 5)], (q_s, q_r), 2 * n + x)
        for i, part in enumerate((pbuf.at[:, 0], pz.at[:, :, 0], pfar.at[:, 0])):
            left(part, (pb_s, pb_r), i)

    for copy in sent:
        copy.wait_send()


def hand_over(*refs):
    n = len(refs) // 2
    sems = refs[-1]
    copies = [pltpu.make_async_copy(refs[i], refs[n + i], sems.at[i]) for i in range(n)]
    for copy in copies:
        copy.start()
    for copy in copies:
        copy.wait()


def on_device(inputs, kv_grads, weight, master, row_state, col_state):
    hbm = pl.BlockSpec(memory_space=pltpu.HBM)
    anywhere = pl.BlockSpec(memory_space=pl.ANY)
    vmem = pl.BlockSpec(memory_space=pltpu.VMEM)
    dma = pltpu.SemaphoreType.DMA
    out_shape = (
        jax.ShapeDtypeStruct((1, 1, 32, 256), F32),
        jax.ShapeDtypeStruct((1, 1, 1, 32), F32),
        jax.ShapeDtypeStruct((1, 256), F32),
        jax.ShapeDtypeStruct((1024, 256), BF),
        jax.ShapeDtypeStruct((1024, 512), BF),
    )
    results = pl.pallas_call(
        kernel,
        out_shape=out_shape,
        in_specs=[hbm] * 6,
        out_specs=(vmem,) * 5,
        scratch_shapes=[
            pltpu.VMEM((1, 1, 32, 256), F32),
            pltpu.VMEM((1, 1, 1, 32), F32),
            pltpu.VMEM((1, 256), F32),
            pltpu.VMEM((1024, 1024), BF),
            pltpu.VMEM((1024, 256), BF),
            pltpu.VMEM((1024, 256), BF),
            pltpu.VMEM((1024, 256), BF),
            pltpu.VMEM((512, 256), BF),
            pltpu.VMEM((1024, 256), F32),
            pltpu.VMEM((5, 2 * B, 256), BF),
            pltpu.VMEM((5, 2 * B, 256), BF),
            pltpu.VMEM((5, 3 * B, 256), BF),
            pltpu.VMEM((5, 3 * B, 256), BF),
            pltpu.VMEM((2, B, 256), BF),
            pltpu.VMEM((2, B, 256), BF),
            pltpu.VMEM((4, B, 256), BF),
            pltpu.VMEM((4, B, 256), BF),
            pltpu.VMEM((1024, 256), BF),
            pltpu.VMEM((10, 2, B, 256), BF),
            pltpu.VMEM((2, 10, 2, B, 256), BF),
            pltpu.VMEM((2, 2, B, 256), BF),
            pltpu.VMEM((16, 5, 128), F32),
            pltpu.VMEM((16, 5, 128), F32),
            dma((9,)),
        ] + [dma((n,)) for n in (2, 5, 5, 2, 4, 4, 25, 2, 1, 4, 1, 4, 2, 3, 15, 15) for _ in range(2)] + [
            pltpu.SemaphoreType.REGULAR] + [pltpu.SemaphoreType.REGULAR] * 3,
        compiler_params=pltpu.CompilerParams(
            collective_id=0, has_side_effects=True, vmem_limit_bytes=24 << 20
        ),
        name="kv_backward_adafactor",
    )(*[pltpu.with_memory_space_constraint(x, pltpu.HBM) for x in (inputs, kv_grads, weight, master, row_state, col_state)])
    return pl.pallas_call(
        hand_over,
        out_shape=out_shape,
        in_specs=[anywhere] * 5,
        out_specs=(hbm,) * 5,
        scratch_shapes=[dma((5,))],
        compiler_params=pltpu.CompilerParams(vmem_limit_bytes=16 << 20),
        name="hand_over",
    )(*results)


def solution(mesh):
    placed = (
        P("dp", "mrow"),
        P("dp", "mcol"),
        P("mrow", "mcol"),
        P("mrow", "dp", None, "mcol"),
        P("mcol", "mrow", "dp", None),
        P("mcol", None),
    )
    return jax.shard_map(
        on_device,
        mesh=mesh,
        in_specs=placed,
        out_specs=(
            P("mrow", "dp", None, "mcol"),
            P("mcol", "mrow", "dp", None),
            P("mcol", None),
            P("mrow", "mcol"),
            P("dp", ("mrow", "mcol")),
        ),
        check_vma=False,
    )
```

```python
import jax
import jax.numpy as jnp
from jax import lax
from jax.experimental import pallas as pl
from jax.experimental.pallas import tpu as pltpu
from jax.sharding import PartitionSpec as P

D = 8192
HEAD = 256
MESH = pl.DeviceIdType.MESH
BF = jnp.bfloat16
F32 = jnp.float32

AGG = (-6, 6, -3, 3, 0)
FAR = AGG[:4]
NEAR = ((1, 1), (-1, 1), (1, 0), (-1, 0), (0, 1))
SIDE = ((2, 1), (2, 0))
XY = ((2, 1, 1), (1, 1, 1), (3, 1, 1), (2, 1, 0), (2, 0, 1), (1, 1, 0), (3, 1, 0), (0, 1, 1),
      (2, 0, 0), (1, 0, 1), (3, 0, 1), (0, 1, 0), (1, 0, 0), (3, 0, 0), (0, 0, 1))
ZS = (8, 7, 9, 6, 10, 5, 11, 4, 12, 3, 13, 2, 14, 1, 15)
B = 32


def kernel(a_hbm, kv_hbm, w_hbm, m_hbm, r_hbm, c_hbm,
           nm_ref, nr_ref, nc_ref, nw_ref, ig_ref,
           m_ref, r_ref, c_ref, a_v, kv, kvo, w_v, wo, grad,
           f_out, f_in, n_out, n_in, side_out, side_in, s2_out, s2_in,
           hbuf, pbuf, pz, pfar, st1, st2, loc, core_s, core_r,
           f_s, f_r, n_s, n_r, side_s, side_r, b_s, b_r, c_s, c_r, d_s, d_r, e_s, e_r,
           po_s, po_r, p_s, p_r, px_s, px_r, q_s, q_r, qf_s, qf_r, pb_s, pb_r, x_s, x_r, z_s, z_r, known3, known6, plane1, plane2):
    dp = lax.axis_index("dp")
    mrow = lax.axis_index("mrow")
    core = lax.axis_index("mcol")
    z, xh = lax.div(dp, 2), lax.rem(dp, 2)
    y, xl = lax.div(mrow, 2), lax.rem(mrow, 2)
    at_x = (xh, 1 - xh)
    at_l = (xl, 1 - xl)
    at_z = [z] + [lax.rem(z + d, 16) for d in range(1, 16)]
    at_y = [y] + [lax.rem(y + d, 4) for d in range(1, 4)]
    at_dp = [[at_z[d] * 2 + at_x[x] for x in range(2)] for d in range(16)]
    at_mrow = [[at_y[d] * 2 + at_l[l] for l in range(2)] for d in range(4)]
    at_core = (core, 1 - core)
    at_rows = [[pl.multiple_of(at_dp[d][x] * B, B) for x in range(2)] for d in range(16)]

    def dev(dz=0, dx=0, dy=0, dl=0, dc=0):
        return at_dp[dz % 16][dx], at_mrow[dy % 4][dl], at_core[dc]

    def rows(dz, dx):
        return pl.ds(at_rows[dz % 16][dx], B)

    sent = []

    def send(src, dst, sems, n, to, later=None):
        copy = pltpu.make_async_remote_copy(
            src_ref=src, dst_ref=dst, send_sem=sems[0].at[n], recv_sem=sems[1].at[n],
            device_id=to, device_id_type=MESH,
        )
        copy.start()
        if later is None:
            sent.append(copy)

    def left(src, sems, n):
        pltpu.make_async_remote_copy(
            src_ref=src, dst_ref=src, send_sem=sems[0].at[n], recv_sem=sems[1].at[n],
            device_id=dev(dc=1), device_id_type=MESH,
        ).wait_send()

    def arrived(dst, sems, n):
        pltpu.make_async_remote_copy(
            src_ref=dst, dst_ref=dst, send_sem=sems[0].at[n], recv_sem=sems[1].at[n],
            device_id=dev(dc=1), device_id_type=MESH,
        ).wait_recv()

    loads = [
        pltpu.make_async_copy(src, dst, loc.at[i])
        for i, (src, dst) in enumerate(
            ((kv_hbm, kv), (w_hbm, w_v), (m_hbm, m_ref), (r_hbm, r_ref), (c_hbm, c_ref)))
    ]
    chunks = [pl.ds(i * 256, 256) for i in range(4)]
    loads_a = [pltpu.make_async_copy(a_hbm.at[:, c], a_v.at[:, c], loc.at[5 + i]) for i, c in enumerate(chunks)]
    loads[0].start()
    for copy in loads_a + loads[1:]:
        copy.start()

    peers = [dev(dz=d, dx=x) for d in (1, -1, 2, -2) for x in (0, 1)]
    peers += [dev(dz=d) for d in (3, -3)]
    peers += [dev(dx=1), dev(dy=1), dev(dy=-1), dev(dl=1), dev(dc=1)]
    barrier = pltpu.get_barrier_semaphore()
    for to in peers:
        pl.semaphore_signal(barrier, inc=1, device_id=to, device_id_type=MESH)

    loads[0].wait()
    for copy, c in zip(loads_a, chunks):
        copy.wait()
        grad[c, :] = lax.dot_general(
            a_v[:, c], kv[...], (((0,), (0,)), ((), ())), preferred_element_type=F32
        )
    for n, (o, x) in enumerate(SIDE):
        side_out[n] = grad[rows(-o - 6, x), :].astype(BF)
    for n, (o, x) in enumerate(NEAR):
        for j in range(2):
            f_out[n, j * B:(j + 1) * B, :] = grad[rows(o - AGG[j], x), :].astype(BF)
        for j in range(3):
            n_out[n, j * B:(j + 1) * B, :] = grad[rows(o - AGG[2 + j], x), :].astype(BF)

    for copy in loads[1:]:
        copy.wait()
    pl.semaphore_wait(barrier, len(peers))

    for n, (o, x) in enumerate(SIDE):
        send(side_out.at[n], side_in.at[n], (side_s, side_r), n, dev(dz=-o, dx=x))
    for n, (o, x) in enumerate(NEAR):
        send(f_out.at[n], f_in.at[n], (f_s, f_r), n, dev(dz=o, dx=x))
    for d in (3, -3):
        pl.semaphore_signal(known3, inc=1, device_id=dev(dz=d), device_id_type=MESH)
    for to in (dev(dy=1), dev(dy=-1), dev(dl=1), dev(dx=1)):
        pl.semaphore_signal(plane1, inc=1, device_id=to, device_id_type=MESH)
    for n, (o, x) in enumerate(NEAR):
        send(n_out.at[n], n_in.at[n], (n_s, n_r), n, dev(dz=o, dx=x))

    params = m_ref[0, 0]
    pbuf[4, core] = params.astype(BF)

    @pl.when(core == 0)
    def _():
        send(pbuf.at[4, 0], pbuf.at[4, 0], (po_s, po_r), 0, dev(dc=1), ())
        left(pbuf.at[4, 0], (po_s, po_r), 0)

    pl.semaphore_wait(known3, 2)
    for d in (6, -6):
        pl.semaphore_signal(known6, inc=1, device_id=dev(dz=d), device_id_type=MESH)

    @pl.when(core == 1)
    def _():
        arrived(pbuf.at[4, 0], (po_s, po_r), 0)
        for j, a in enumerate(FAR):
            send(pbuf.at[4], pbuf.at[j], (p_s, p_r), j, dev(dz=a), ())

    pl.semaphore_wait(plane1, 4)
    for d in (1, -1, 2):
        pl.semaphore_signal(plane2, inc=1, device_id=dev(dy=d), device_id_type=MESH)
    half = w_v.shape[0] // 2
    mine = pl.ds(pl.multiple_of(core * half, half), half)
    theirs = pl.ds(pl.multiple_of((1 - core) * half, half), half)
    send(kv, kvo, (core_s, core_r), 0, dev(dc=1))
    send(w_v.at[theirs], wo, (core_s, core_r), 1, dev(dc=1))

    def aggregate(j):
        a = AGG[j]
        part = grad[rows(-a, 0), :]
        for n in range(5):
            got = f_in[n, j * B:(j + 1) * B, :] if j < 2 else n_in[n, (j - 2) * B:(j - 1) * B, :]
            part = part + got.astype(F32)
        if a == 6:
            for n in range(2):
                part = part + side_in[n].astype(F32)
        if a == 0:
            return part
        s2_out[j] = part.astype(BF)
        send(s2_out.at[j], s2_in.at[j], (b_s, b_r), j, dev(dz=-a))

    for n in range(2):
        arrived(side_in.at[n], (side_s, side_r), n)
    for n in range(5):
        arrived(f_in.at[n], (f_s, f_r), n)
    aggregate(0)
    aggregate(1)
    for n in range(5):
        arrived(n_in.at[n], (n_s, n_r), n)
    aggregate(2)
    aggregate(3)
    total = aggregate(4)

    @pl.when(core == 1)
    def _():
        for j in range(4):
            arrived(pbuf.at[j], (p_s, p_r), j)
        send(pbuf.at[pl.ds(0, 5)], pbuf.at[pl.ds(5, 5)], (px_s, px_r), 0, dev(dx=1), ())

    def third(x):
        if x == 1:
            arrived(pbuf.at[pl.ds(5, 5)], (px_s, px_r), 0)
        send(pbuf.at[5 * x + 1], pfar.at[x], (qf_s, qf_r), x, dev(dz=2), ())
        for n, o in enumerate((1, -1)):
            part = pl.ds(5 * x, 5)
            send(pbuf.at[part], pz.at[n, part], (q_s, q_r), 2 * n + x, dev(dz=o), ())

    @pl.when(core == 1)
    def _():
        third(0)

    arrived(kvo, (core_s, core_r), 0)
    arrived(wo, (core_s, core_r), 1)

    def ig_step(i, _):
        toks = pl.ds(pl.multiple_of(i * 256, 256), 256)
        dims = (((1,), (1,)), ((), ()))
        own = lax.dot_general(kv[toks, :], w_v[mine, :], dims, preferred_element_type=F32).astype(BF)
        other = lax.dot_general(kvo[toks, :], wo[...], dims, preferred_element_type=F32).astype(BF)
        ig_ref[toks, :] = (own.astype(F32) + other.astype(F32)).astype(BF)
        return 0

    lax.fori_loop(0, 4, ig_step, 0)
    for copy in sent:
        copy.wait_send()
    sent.clear()
    for j in (2, 3, 0, 1):
        arrived(s2_in.at[j], (b_s, b_r), j)
        total = total + s2_in[j].astype(F32)
    g = total

    eye = (lax.broadcasted_iota(jnp.int32, (B, B), 0) == lax.broadcasted_iota(jnp.int32, (B, B), 1)).astype(F32)
    old_rows = jnp.sum(eye * r_ref[0, 0], axis=1, keepdims=True)
    sq = g * g + 1e-30
    new_rows = 0.8 * old_rows + 0.2 * (jnp.sum(sq, axis=1, keepdims=True) * (1.0 / HEAD))
    h = g / jnp.sqrt(new_rows)
    hbuf[rows(0, 0), :] = h.astype(BF)
    col = jnp.sum(sq, axis=0, keepdims=True)
    weighted = jnp.sum(h * h, axis=0, keepdims=True)
    pl.semaphore_wait(plane2, 3)
    my_xy = y * 4 + xh * 2 + xl
    low = lax.broadcasted_iota(jnp.int32, (1, 128), 1) < 64
    st1[my_xy] = jnp.concatenate(
        [col[:, :128], col[:, 128:], weighted[:, :128], weighted[:, 128:],
         jnp.where(low, jnp.sum(new_rows), jnp.sum(params * params))], axis=0)
    for n, (py, ph, pl_) in enumerate(XY):
        send(st1.at[my_xy], st1.at[my_xy], (x_s, x_r), n, dev(dy=py, dx=ph, dl=pl_))

    for j, a in enumerate(FAR):
        send(hbuf.at[rows(0, 0)], hbuf.at[rows(0, 0)], (c_s, c_r), j, dev(dz=a))

    def forward(j):
        src = hbuf.at[rows(-AGG[j], 0)]
        for n, (o, x) in enumerate(NEAR):
            send(src, src, (d_s, d_r), j * 5 + n, dev(dz=o, dx=x))
        if AGG[j] == 6:
            for n, (o, x) in enumerate(SIDE):
                send(src, src, (e_s, e_r), n, dev(dz=o, dx=x))

    forward(4)
    @pl.when(core == 1)
    def _():
        third(1)

    nr_ref[0, 0] = jnp.sum(eye * new_rows, axis=0, keepdims=True)
    pl.semaphore_wait(known6, 2)
    for j in (2, 3):
        arrived(hbuf.at[rows(-AGG[j], 0)], (c_s, c_r), j)
        forward(j)
    for n, (py, ph, pl_) in enumerate(XY):
        src = at_y[-py % 4] * 4 + at_x[ph] * 2 + at_l[pl_]
        arrived(st1.at[src], (x_s, x_r), n)
    plane = st1[0]
    for i in range(1, 16):
        plane = plane + st1[i]
    st2[z] = plane
    early = len(sent)
    for n, d in enumerate(ZS):
        send(st2.at[z], st2.at[z], (z_s, z_r), n, dev(dz=d))
    for j in (0, 1):
        arrived(hbuf.at[rows(-AGG[j], 0)], (c_s, c_r), j)
        forward(j)

    for copy in sent[:early]:
        copy.wait_send()
    del sent[:early]
    @pl.when(core == 1)
    def _():
        for x in range(2):
            arrived(pfar.at[x], (qf_s, qf_r), x)
            for n in range(2):
                arrived(pz.at[n, pl.ds(5 * x, 5)], (q_s, q_r), 2 * n + x)
        for i, part in enumerate((pbuf.at[:, 0], pz.at[:, :, 0], pfar.at[:, 0])):
            send(part, part, (pb_s, pb_r), i, dev(dc=1), ())

    for j in (4, 2, 3):
        for n, (o, x) in enumerate(NEAR):
            arrived(hbuf.at[rows(-o - AGG[j], x)], (d_s, d_r), j * 5 + n)
    for n, d in enumerate(ZS):
        arrived(st2.at[at_z[-d % 16]], (z_s, z_r), n)
    whole = st2[0]
    for i in range(1, 16):
        whole = whole + st2[i]
    col_sum = jnp.concatenate([whole[0:1], whole[1:2]], axis=1)
    weight_sum = jnp.concatenate([whole[2:3], whole[3:4]], axis=1)
    row_avg = whole[4:5, 0:1] / D
    param_rms = jnp.sqrt(whole[4:5, 64:65] / (D * HEAD))
    new_cols = 0.8 * c_ref[...] + 0.2 * col_sum / D
    nc_ref[...] = new_cols
    update_sq = row_avg * jnp.sum(weight_sum / new_cols, axis=1, keepdims=True)
    clip = jnp.maximum(1.0, jnp.sqrt(update_sq / (D * HEAD)))
    scale = (0.5 * param_rms / clip) * (jnp.sqrt(row_avg) / jnp.sqrt(new_cols))
    nm_ref[0, 0] = params - h * scale

    for j in range(2):
        for n, (o, x) in enumerate(NEAR):
            arrived(hbuf.at[rows(-o - AGG[j], x)], (d_s, d_r), j * 5 + n)
    for n, (o, x) in enumerate(SIDE):
        arrived(hbuf.at[rows(-o - 6, x)], (e_s, e_r), n)
    for i in range(3):
        @pl.when(core == 0)
        def _():
            arrived((pbuf.at[:, 0], pz.at[:, :, 0], pfar.at[:, 0])[i], (pb_s, pb_r), i)

    def finish(p, index):
        nw_ref[index, :] = (p.astype(F32) - hbuf[index, :].astype(F32) * scale).astype(BF)

    for x in range(2):
        for j, a in enumerate(AGG):
            finish(pbuf[5 * x + j, core], rows(-a, x))
            for n, o in enumerate((1, -1)):
                finish(pz[n, 5 * x + j, core], rows(-o - a, x))
        finish(pfar[x, core], rows(-8, x))

    @pl.when(core == 1)
    def _():
        for j in range(4):
            left(pbuf.at[j], (p_s, p_r), j)
        left(pbuf.at[pl.ds(0, 5)], (px_s, px_r), 0)
        for x in range(2):
            left(pfar.at[x], (qf_s, qf_r), x)
            for n in range(2):
                left(pz.at[n, pl.ds(5 * x, 5)], (q_s, q_r), 2 * n + x)
        for i, part in enumerate((pbuf.at[:, 0], pz.at[:, :, 0], pfar.at[:, 0])):
            left(part, (pb_s, pb_r), i)

    for copy in sent:
        copy.wait_send()


def hand_over(*refs):
    n = len(refs) // 2
    sems = refs[-1]
    copies = []
    for src, dst in zip(refs[:n], refs[n:-1]):
        parts = 4 if src.shape[0] == 1024 else 1
        for i in range(parts):
            piece = pl.ds(i * (src.shape[0] // parts), src.shape[0] // parts)
            copies.append(pltpu.make_async_copy(src.at[piece], dst.at[piece], sems.at[len(copies)]))
            copies[-1].start()
    for copy in copies:
        copy.wait()


def on_device(inputs, kv_grads, weight, master, row_state, col_state):
    hbm = pl.BlockSpec(memory_space=pltpu.HBM)
    anywhere = pl.BlockSpec(memory_space=pl.ANY)
    vmem = pl.BlockSpec(memory_space=pltpu.VMEM)
    dma = pltpu.SemaphoreType.DMA
    out_shape = (
        jax.ShapeDtypeStruct((1, 1, 32, 256), F32),
        jax.ShapeDtypeStruct((1, 1, 1, 32), F32),
        jax.ShapeDtypeStruct((1, 256), F32),
        jax.ShapeDtypeStruct((1024, 256), BF),
        jax.ShapeDtypeStruct((1024, 512), BF),
    )
    results = pl.pallas_call(
        kernel,
        out_shape=out_shape,
        in_specs=[hbm] * 6,
        out_specs=(vmem,) * 5,
        scratch_shapes=[
            pltpu.VMEM((1, 1, 32, 256), F32),
            pltpu.VMEM((1, 1, 1, 32), F32),
            pltpu.VMEM((1, 256), F32),
            pltpu.VMEM((1024, 1024), BF),
            pltpu.VMEM((1024, 256), BF),
            pltpu.VMEM((1024, 256), BF),
            pltpu.VMEM((1024, 256), BF),
            pltpu.VMEM((512, 256), BF),
            pltpu.VMEM((1024, 256), F32),
            pltpu.VMEM((5, 2 * B, 256), BF),
            pltpu.VMEM((5, 2 * B, 256), BF),
            pltpu.VMEM((5, 3 * B, 256), BF),
            pltpu.VMEM((5, 3 * B, 256), BF),
            pltpu.VMEM((2, B, 256), BF),
            pltpu.VMEM((2, B, 256), BF),
            pltpu.VMEM((4, B, 256), BF),
            pltpu.VMEM((4, B, 256), BF),
            pltpu.VMEM((1024, 256), BF),
            pltpu.VMEM((10, 2, B, 256), BF),
            pltpu.VMEM((2, 10, 2, B, 256), BF),
            pltpu.VMEM((2, 2, B, 256), BF),
            pltpu.VMEM((16, 5, 128), F32),
            pltpu.VMEM((16, 5, 128), F32),
            dma((9,)),
        ] + [dma((n,)) for n in (2, 5, 5, 2, 4, 4, 25, 2, 1, 4, 1, 4, 2, 3, 15, 15) for _ in range(2)] + [
            pltpu.SemaphoreType.REGULAR] + [pltpu.SemaphoreType.REGULAR] * 3,
        compiler_params=pltpu.CompilerParams(
            collective_id=0, has_side_effects=True, vmem_limit_bytes=24 << 20
        ),
        name="kv_backward_adafactor",
    )(*[pltpu.with_memory_space_constraint(x, pltpu.HBM) for x in (inputs, kv_grads, weight, master, row_state, col_state)])
    return pl.pallas_call(
        hand_over,
        out_shape=out_shape,
        in_specs=[anywhere] * 5,
        out_specs=(hbm,) * 5,
        scratch_shapes=[dma((11,))],
        compiler_params=pltpu.CompilerParams(vmem_limit_bytes=16 << 20),
        name="hand_over",
    )(*results)


def solution(mesh):
    placed = (
        P("dp", "mrow"),
        P("dp", "mcol"),
        P("mrow", "mcol"),
        P("mrow", "dp", None, "mcol"),
        P("mcol", "mrow", "dp", None),
        P("mcol", None),
    )
    return jax.shard_map(
        on_device,
        mesh=mesh,
        in_specs=placed,
        out_specs=(
            P("mrow", "dp", None, "mcol"),
            P("mcol", "mrow", "dp", None),
            P("mcol", None),
            P("mrow", "mcol"),
            P("dp", ("mrow", "mcol")),
        ),
        check_vma=False,
    )
```

```python
import jax
import jax.numpy as jnp
from jax import lax
from jax.experimental import pallas as pl
from jax.experimental.pallas import tpu as pltpu
from jax.sharding import PartitionSpec as P

D = 8192
HEAD = 256
MESH = pl.DeviceIdType.MESH
BF = jnp.bfloat16
F32 = jnp.float32

AGG = (-6, 6, -3, 3, 0)
FAR = AGG[:4]
NEAR = ((1, 1), (-1, 1), (1, 0), (-1, 0), (0, 1))
SIDE = ((2, 1), (2, 0))
XY = ((2, 1, 1), (1, 1, 1), (3, 1, 1), (2, 1, 0), (2, 0, 1), (1, 1, 0), (3, 1, 0), (0, 1, 1),
      (2, 0, 0), (1, 0, 1), (3, 0, 1), (0, 1, 0), (1, 0, 0), (3, 0, 0), (0, 0, 1))
ZS = (8, 7, 9, 6, 10, 5, 11, 4, 12, 3, 13, 2, 14, 1, 15)
B = 32


def kernel(a_hbm, kv_hbm, w_hbm, m_hbm, r_hbm, c_hbm,
           nm_ref, nr_ref, nc_ref, nw_ref, ig_ref,
           m_ref, r_ref, c_ref, a_v, kv, kvo, w_v, wo, grad,
           f_out, f_in, n_out, n_in, side_out, side_in, s2_out, s2_in,
           hbuf, pbuf, pz, pfar, st1, st2, loc, core_s, core_r,
           f_s, f_r, n_s, n_r, side_s, side_r, b_s, b_r, c_s, c_r, d_s, d_r, e_s, e_r,
           po_s, po_r, p_s, p_r, px_s, px_r, q_s, q_r, qf_s, qf_r, pb_s, pb_r, x_s, x_r, z_s, z_r, known3, known6, plane1, plane2):
    dp = lax.axis_index("dp")
    mrow = lax.axis_index("mrow")
    core = lax.axis_index("mcol")
    z, xh = lax.div(dp, 2), lax.rem(dp, 2)
    y, xl = lax.div(mrow, 2), lax.rem(mrow, 2)
    at_x = (xh, 1 - xh)
    at_l = (xl, 1 - xl)
    at_z = [z] + [lax.rem(z + d, 16) for d in range(1, 16)]
    at_y = [y] + [lax.rem(y + d, 4) for d in range(1, 4)]
    at_dp = [[at_z[d] * 2 + at_x[x] for x in range(2)] for d in range(16)]
    at_mrow = [[at_y[d] * 2 + at_l[l] for l in range(2)] for d in range(4)]
    at_core = (core, 1 - core)
    at_rows = [[pl.multiple_of(at_dp[d][x] * B, B) for x in range(2)] for d in range(16)]

    def dev(dz=0, dx=0, dy=0, dl=0, dc=0):
        return at_dp[dz % 16][dx], at_mrow[dy % 4][dl], at_core[dc]

    def rows(dz, dx):
        return pl.ds(at_rows[dz % 16][dx], B)

    sent = []

    def send(src, dst, sems, n, to, later=None):
        copy = pltpu.make_async_remote_copy(
            src_ref=src, dst_ref=dst, send_sem=sems[0].at[n], recv_sem=sems[1].at[n],
            device_id=to, device_id_type=MESH,
        )
        copy.start()
        if later is None:
            sent.append(copy)

    def left(src, sems, n):
        pltpu.make_async_remote_copy(
            src_ref=src, dst_ref=src, send_sem=sems[0].at[n], recv_sem=sems[1].at[n],
            device_id=dev(dc=1), device_id_type=MESH,
        ).wait_send()

    def arrived(dst, sems, n):
        pltpu.make_async_remote_copy(
            src_ref=dst, dst_ref=dst, send_sem=sems[0].at[n], recv_sem=sems[1].at[n],
            device_id=dev(dc=1), device_id_type=MESH,
        ).wait_recv()

    loads = [
        pltpu.make_async_copy(src, dst, loc.at[i])
        for i, (src, dst) in enumerate(
            ((kv_hbm, kv), (w_hbm, w_v), (m_hbm, m_ref), (r_hbm, r_ref), (c_hbm, c_ref)))
    ]
    chunks = [pl.ds(i * 256, 256) for i in range(4)]
    loads_a = [pltpu.make_async_copy(a_hbm.at[:, c], a_v.at[:, c], loc.at[5 + i]) for i, c in enumerate(chunks)]
    loads[0].start()
    for copy in loads_a + loads[1:]:
        copy.start()

    peers = [dev(dz=d, dx=x) for d in (1, -1, 2, -2) for x in (0, 1)]
    peers += [dev(dz=d) for d in (3, -3)]
    peers += [dev(dx=1), dev(dy=1), dev(dy=-1), dev(dl=1), dev(dc=1)]
    barrier = pltpu.get_barrier_semaphore()
    for to in peers:
        pl.semaphore_signal(barrier, inc=1, device_id=to, device_id_type=MESH)

    loads[0].wait()
    for copy, c in zip(loads_a, chunks):
        copy.wait()
        grad[c, :] = lax.dot_general(
            a_v[:, c], kv[...], (((0,), (0,)), ((), ())), preferred_element_type=F32
        )
    for n, (o, x) in enumerate(SIDE):
        side_out[n] = grad[rows(-o - 6, x), :].astype(BF)
    for n, (o, x) in enumerate(NEAR):
        for j in range(2):
            f_out[n, j * B:(j + 1) * B, :] = grad[rows(o - AGG[j], x), :].astype(BF)
        for j in range(3):
            n_out[n, j * B:(j + 1) * B, :] = grad[rows(o - AGG[2 + j], x), :].astype(BF)

    for copy in loads[1:]:
        copy.wait()
    pl.semaphore_wait(barrier, len(peers))

    for n, (o, x) in enumerate(SIDE):
        send(side_out.at[n], side_in.at[n], (side_s, side_r), n, dev(dz=-o, dx=x))
    for n, (o, x) in enumerate(NEAR):
        send(f_out.at[n], f_in.at[n], (f_s, f_r), n, dev(dz=o, dx=x))
    for d in (3, -3):
        pl.semaphore_signal(known3, inc=1, device_id=dev(dz=d), device_id_type=MESH)
    for to in (dev(dy=1), dev(dy=-1), dev(dl=1), dev(dx=1)):
        pl.semaphore_signal(plane1, inc=1, device_id=to, device_id_type=MESH)
    for n, (o, x) in enumerate(NEAR):
        send(n_out.at[n], n_in.at[n], (n_s, n_r), n, dev(dz=o, dx=x))

    params = m_ref[0, 0]
    pbuf[4, core] = params.astype(BF)

    @pl.when(core == 0)
    def _():
        send(pbuf.at[4, 0], pbuf.at[4, 0], (po_s, po_r), 0, dev(dc=1), ())
        left(pbuf.at[4, 0], (po_s, po_r), 0)

    pl.semaphore_wait(known3, 2)
    for d in (6, -6):
        pl.semaphore_signal(known6, inc=1, device_id=dev(dz=d), device_id_type=MESH)

    @pl.when(core == 1)
    def _():
        arrived(pbuf.at[4, 0], (po_s, po_r), 0)
        for j, a in enumerate(FAR):
            send(pbuf.at[4], pbuf.at[j], (p_s, p_r), j, dev(dz=a), ())

    pl.semaphore_wait(plane1, 4)
    for d in (1, -1, 2):
        pl.semaphore_signal(plane2, inc=1, device_id=dev(dy=d), device_id_type=MESH)
    half = w_v.shape[0] // 2
    mine = pl.ds(pl.multiple_of(core * half, half), half)
    theirs = pl.ds(pl.multiple_of((1 - core) * half, half), half)

    def aggregate(j):
        a = AGG[j]
        part = grad[rows(-a, 0), :]
        for n in range(5):
            got = f_in[n, j * B:(j + 1) * B, :] if j < 2 else n_in[n, (j - 2) * B:(j - 1) * B, :]
            part = part + got.astype(F32)
        if a == 6:
            for n in range(2):
                part = part + side_in[n].astype(F32)
        if a == 0:
            return part
        s2_out[j] = part.astype(BF)
        send(s2_out.at[j], s2_in.at[j], (b_s, b_r), j, dev(dz=-a))

    for n in range(2):
        arrived(side_in.at[n], (side_s, side_r), n)
    for n in range(5):
        arrived(f_in.at[n], (f_s, f_r), n)
    aggregate(0)
    aggregate(1)
    send(kv, kvo, (core_s, core_r), 0, dev(dc=1))
    send(w_v.at[theirs], wo, (core_s, core_r), 1, dev(dc=1))
    for n in range(5):
        arrived(n_in.at[n], (n_s, n_r), n)
    aggregate(2)
    aggregate(3)
    total = aggregate(4)

    @pl.when(core == 1)
    def _():
        for j in range(4):
            arrived(pbuf.at[j], (p_s, p_r), j)
        send(pbuf.at[pl.ds(0, 5)], pbuf.at[pl.ds(5, 5)], (px_s, px_r), 0, dev(dx=1), ())

    def third(x):
        if x == 1:
            arrived(pbuf.at[pl.ds(5, 5)], (px_s, px_r), 0)
        send(pbuf.at[5 * x + 1], pfar.at[x], (qf_s, qf_r), x, dev(dz=2), ())
        for n, o in enumerate((1, -1)):
            part = pl.ds(5 * x, 5)
            send(pbuf.at[part], pz.at[n, part], (q_s, q_r), 2 * n + x, dev(dz=o), ())

    @pl.when(core == 1)
    def _():
        third(0)

    arrived(kvo, (core_s, core_r), 0)
    arrived(wo, (core_s, core_r), 1)

    def ig_step(i, _):
        toks = pl.ds(pl.multiple_of(i * 256, 256), 256)
        dims = (((1,), (1,)), ((), ()))
        own = lax.dot_general(kv[toks, :], w_v[mine, :], dims, preferred_element_type=F32).astype(BF)
        other = lax.dot_general(kvo[toks, :], wo[...], dims, preferred_element_type=F32).astype(BF)
        ig_ref[toks, :] = (own.astype(F32) + other.astype(F32)).astype(BF)
        return 0

    lax.fori_loop(0, 4, ig_step, 0)
    for copy in sent:
        copy.wait_send()
    sent.clear()
    for j in (2, 3, 0, 1):
        arrived(s2_in.at[j], (b_s, b_r), j)
        total = total + s2_in[j].astype(F32)
    g = total

    eye = (lax.broadcasted_iota(jnp.int32, (B, B), 0) == lax.broadcasted_iota(jnp.int32, (B, B), 1)).astype(F32)
    old_rows = jnp.sum(eye * r_ref[0, 0], axis=1, keepdims=True)
    sq = g * g + 1e-30
    new_rows = 0.8 * old_rows + 0.2 * (jnp.sum(sq, axis=1, keepdims=True) * (1.0 / HEAD))
    h = g / jnp.sqrt(new_rows)
    hbuf[rows(0, 0), :] = h.astype(BF)
    col = jnp.sum(sq, axis=0, keepdims=True)
    weighted = jnp.sum(h * h, axis=0, keepdims=True)
    pl.semaphore_wait(plane2, 3)
    my_xy = y * 4 + xh * 2 + xl
    low = lax.broadcasted_iota(jnp.int32, (1, 128), 1) < 64
    st1[my_xy] = jnp.concatenate(
        [col[:, :128], col[:, 128:], weighted[:, :128], weighted[:, 128:],
         jnp.where(low, jnp.sum(new_rows), jnp.sum(params * params))], axis=0)
    for n, (py, ph, pl_) in enumerate(XY):
        send(st1.at[my_xy], st1.at[my_xy], (x_s, x_r), n, dev(dy=py, dx=ph, dl=pl_))

    for j, a in enumerate(FAR):
        send(hbuf.at[rows(0, 0)], hbuf.at[rows(0, 0)], (c_s, c_r), j, dev(dz=a))

    def forward(j):
        src = hbuf.at[rows(-AGG[j], 0)]
        for n, (o, x) in enumerate(NEAR):
            send(src, src, (d_s, d_r), j * 5 + n, dev(dz=o, dx=x))
        if AGG[j] == 6:
            for n, (o, x) in enumerate(SIDE):
                send(src, src, (e_s, e_r), n, dev(dz=o, dx=x))

    forward(4)
    @pl.when(core == 1)
    def _():
        third(1)

    nr_ref[0, 0] = jnp.sum(eye * new_rows, axis=0, keepdims=True)
    pl.semaphore_wait(known6, 2)
    for j in (2, 3):
        arrived(hbuf.at[rows(-AGG[j], 0)], (c_s, c_r), j)
        forward(j)
    for n, (py, ph, pl_) in enumerate(XY):
        src = at_y[-py % 4] * 4 + at_x[ph] * 2 + at_l[pl_]
        arrived(st1.at[src], (x_s, x_r), n)
    plane = st1[0]
    for i in range(1, 16):
        plane = plane + st1[i]
    st2[z] = plane
    early = len(sent)
    for n, d in enumerate(ZS):
        send(st2.at[z], st2.at[z], (z_s, z_r), n, dev(dz=d))
    for j in (0, 1):
        arrived(hbuf.at[rows(-AGG[j], 0)], (c_s, c_r), j)
        forward(j)

    for copy in sent[:early]:
        copy.wait_send()
    del sent[:early]
    @pl.when(core == 1)
    def _():
        for x in range(2):
            arrived(pfar.at[x], (qf_s, qf_r), x)
            for n in range(2):
                arrived(pz.at[n, pl.ds(5 * x, 5)], (q_s, q_r), 2 * n + x)
        for i, part in enumerate((pbuf.at[:, 0], pz.at[:, :, 0], pfar.at[:, 0])):
            send(part, part, (pb_s, pb_r), i, dev(dc=1), ())

    for j in (4, 2, 3):
        for n, (o, x) in enumerate(NEAR):
            arrived(hbuf.at[rows(-o - AGG[j], x)], (d_s, d_r), j * 5 + n)
    for n, d in enumerate(ZS):
        arrived(st2.at[at_z[-d % 16]], (z_s, z_r), n)
    whole = st2[0]
    for i in range(1, 16):
        whole = whole + st2[i]
    col_sum = jnp.concatenate([whole[0:1], whole[1:2]], axis=1)
    weight_sum = jnp.concatenate([whole[2:3], whole[3:4]], axis=1)
    row_avg = whole[4:5, 0:1] / D
    param_rms = jnp.sqrt(whole[4:5, 64:65] / (D * HEAD))
    new_cols = 0.8 * c_ref[...] + 0.2 * col_sum / D
    nc_ref[...] = new_cols
    update_sq = row_avg * jnp.sum(weight_sum / new_cols, axis=1, keepdims=True)
    clip = jnp.maximum(1.0, jnp.sqrt(update_sq / (D * HEAD)))
    scale = (0.5 * param_rms / clip) * (jnp.sqrt(row_avg) / jnp.sqrt(new_cols))
    nm_ref[0, 0] = params - h * scale

    for j in range(2):
        for n, (o, x) in enumerate(NEAR):
            arrived(hbuf.at[rows(-o - AGG[j], x)], (d_s, d_r), j * 5 + n)
    for n, (o, x) in enumerate(SIDE):
        arrived(hbuf.at[rows(-o - 6, x)], (e_s, e_r), n)
    for i in range(3):
        @pl.when(core == 0)
        def _():
            arrived((pbuf.at[:, 0], pz.at[:, :, 0], pfar.at[:, 0])[i], (pb_s, pb_r), i)

    def finish(p, index):
        nw_ref[index, :] = (p.astype(F32) - hbuf[index, :].astype(F32) * scale).astype(BF)

    for x in range(2):
        for j, a in enumerate(AGG):
            finish(pbuf[5 * x + j, core], rows(-a, x))
            for n, o in enumerate((1, -1)):
                finish(pz[n, 5 * x + j, core], rows(-o - a, x))
        finish(pfar[x, core], rows(-8, x))

    @pl.when(core == 1)
    def _():
        for j in range(4):
            left(pbuf.at[j], (p_s, p_r), j)
        left(pbuf.at[pl.ds(0, 5)], (px_s, px_r), 0)
        for x in range(2):
            left(pfar.at[x], (qf_s, qf_r), x)
            for n in range(2):
                left(pz.at[n, pl.ds(5 * x, 5)], (q_s, q_r), 2 * n + x)
        for i, part in enumerate((pbuf.at[:, 0], pz.at[:, :, 0], pfar.at[:, 0])):
            left(part, (pb_s, pb_r), i)

    for copy in sent:
        copy.wait_send()


def hand_over(*refs):
    n = len(refs) // 2
    sems = refs[-1]
    copies = [pltpu.make_async_copy(refs[i], refs[n + i], sems.at[i]) for i in range(n)]
    for copy in copies:
        copy.start()
    for copy in copies:
        copy.wait()


def on_device(inputs, kv_grads, weight, master, row_state, col_state):
    hbm = pl.BlockSpec(memory_space=pltpu.HBM)
    anywhere = pl.BlockSpec(memory_space=pl.ANY)
    vmem = pl.BlockSpec(memory_space=pltpu.VMEM)
    dma = pltpu.SemaphoreType.DMA
    out_shape = (
        jax.ShapeDtypeStruct((1, 1, 32, 256), F32),
        jax.ShapeDtypeStruct((1, 1, 1, 32), F32),
        jax.ShapeDtypeStruct((1, 256), F32),
        jax.ShapeDtypeStruct((1024, 256), BF),
        jax.ShapeDtypeStruct((1024, 512), BF),
    )
    results = pl.pallas_call(
        kernel,
        out_shape=out_shape,
        in_specs=[hbm] * 6,
        out_specs=(vmem,) * 5,
        scratch_shapes=[
            pltpu.VMEM((1, 1, 32, 256), F32),
            pltpu.VMEM((1, 1, 1, 32), F32),
            pltpu.VMEM((1, 256), F32),
            pltpu.VMEM((1024, 1024), BF),
            pltpu.VMEM((1024, 256), BF),
            pltpu.VMEM((1024, 256), BF),
            pltpu.VMEM((1024, 256), BF),
            pltpu.VMEM((512, 256), BF),
            pltpu.VMEM((1024, 256), F32),
            pltpu.VMEM((5, 2 * B, 256), BF),
            pltpu.VMEM((5, 2 * B, 256), BF),
            pltpu.VMEM((5, 3 * B, 256), BF),
            pltpu.VMEM((5, 3 * B, 256), BF),
            pltpu.VMEM((2, B, 256), BF),
            pltpu.VMEM((2, B, 256), BF),
            pltpu.VMEM((4, B, 256), BF),
            pltpu.VMEM((4, B, 256), BF),
            pltpu.VMEM((1024, 256), BF),
            pltpu.VMEM((10, 2, B, 256), BF),
            pltpu.VMEM((2, 10, 2, B, 256), BF),
            pltpu.VMEM((2, 2, B, 256), BF),
            pltpu.VMEM((16, 5, 128), F32),
            pltpu.VMEM((16, 5, 128), F32),
            dma((9,)),
        ] + [dma((n,)) for n in (2, 5, 5, 2, 4, 4, 25, 2, 1, 4, 1, 4, 2, 3, 15, 15) for _ in range(2)] + [
            pltpu.SemaphoreType.REGULAR] + [pltpu.SemaphoreType.REGULAR] * 3,
        compiler_params=pltpu.CompilerParams(
            collective_id=0, has_side_effects=True, vmem_limit_bytes=24 << 20
        ),
        name="kv_backward_adafactor",
    )(*[pltpu.with_memory_space_constraint(x, pltpu.HBM) for x in (inputs, kv_grads, weight, master, row_state, col_state)])
    return pl.pallas_call(
        hand_over,
        out_shape=out_shape,
        in_specs=[anywhere] * 5,
        out_specs=(hbm,) * 5,
        scratch_shapes=[dma((5,))],
        compiler_params=pltpu.CompilerParams(vmem_limit_bytes=16 << 20),
        name="hand_over",
    )(*results)


def solution(mesh):
    placed = (
        P("dp", "mrow"),
        P("dp", "mcol"),
        P("mrow", "mcol"),
        P("mrow", "dp", None, "mcol"),
        P("mcol", "mrow", "dp", None),
        P("mcol", None),
    )
    return jax.shard_map(
        on_device,
        mesh=mesh,
        in_specs=placed,
        out_specs=(
            P("mrow", "dp", None, "mcol"),
            P("mcol", "mrow", "dp", None),
            P("mcol", None),
            P("mrow", "mcol"),
            P("dp", ("mrow", "mcol")),
        ),
        check_vma=False,
    )
```
